256 devices in a mesh: row: 16 (over z, core), col: 16 (over x, y).
Axes of the slice: x: 4, y: 4, z: 8, core: 2. Of those that a mesh axis runs over, the one named last changes fastest.
Arguments:
- weights: float32 [4096, 28672], P('row', 'col'), may hold values from -6 to 6
- momentum: float32 [4096, 28672], P('row', 'col'), may hold values from -6 to 6
- gradient: bfloat16 [4096, 28672], P('row', 'col'), may hold values from -200 to 200
- right_factor: float32 [512, 28672], P('row', 'col'), may hold values from -6 to 6
Outputs:
- new_weights: float32 [4096, 28672], P('row', 'col')
- new_momentum: float32 [4096, 28672], P('row', 'col')
- new_right: float32 [512, 28672], P('row', 'col')
The draws below stay inside these ranges and needn't reach their ends.
All inputs are finite; a program needn't handle non-finite values.
Results may differ from the reference program's by a relative error of at most 0.0003.
Values sent between devices are 32-bit elements; how exact they have to be, the bound alone decides.
No kernel may reach another device: no remote copies, remote signals or barrier semaphores. Data moves between devices by JAX's collectives and lax.ppermute only.
A program may use at most 64 MiB of HBM per device.

```python
import jax
import jax.numpy as jnp
from jax import lax

M = 4096
N = 28672
R = 512


def draw_gradient(key, part):
    key = jax.random.fold_in(key, 7)
    key_noise, key_spread = jax.random.split(key, 2)
    rising = 3.0 ** (jnp.arange(N, dtype=jnp.float32) / N)
    spread = 10.0 ** jax.random.uniform(key_spread, (N,), jnp.float32)
    values = jax.random.normal(key_noise, (M, N), jnp.float32) * (0.2 * spread * rising)[None, :]
    return jnp.clip(values, -200.0, 200.0).astype(jnp.bfloat16)


def steps_of(key, dims, cuts, low, largest):
    def one(dim, parts):
        heights = jax.random.uniform(jax.random.fold_in(jax.random.fold_in(key, 6), dim), (parts,), jnp.float32, low / len(cuts), largest / len(cuts))
        return jnp.repeat(jnp.exp(heights), dims[dim] // parts).reshape((-1,) + (1,) * (len(dims) - dim - 1))

    gain = one(*cuts[0])
    for cut in cuts[1:]:
        gain = gain * one(*cut)
    return gain


def gaussian(key, shape, scale, limit, cuts=(), kind=jnp.bfloat16):
    loudness = steps_of(key, shape, cuts, -0.22, 0.18) if cuts else 1.0
    values = jax.random.normal(key, shape, jnp.float32) * scale * loudness
    return jnp.minimum(jnp.maximum(values, -limit), limit).astype(kind)


def setup_inputs(seed: int = 0) -> dict:
    seeds = jax.random.split(jax.random.key(seed), 5)
    weights = gaussian(seeds[0], (M, N), 1.0, 6.0, ((0, 16), (1, 16)), jnp.float32)
    momentum = gaussian(seeds[1], (M, N), 1.0, 6.0, ((0, 16), (1, 16)), jnp.float32)
    gradient = draw_gradient(jax.random.fold_in(seeds[4], 71), 0)
    right_factor = gaussian(seeds[3], (R, N), 1.0, 6.0, ((0, 16), (1, 16)), jnp.float32)
    return {"weights": weights, "momentum": momentum, "gradient": gradient, "right_factor": right_factor}


decay_keep = 0.05
step_size = 0.5
eps_norm = 1e-06

def reference(weights, momentum, gradient, right_factor):
    highest = lax.Precision.HIGHEST
    buffer = momentum + gradient.astype(jnp.float32)
    left = jnp.dot(buffer.astype(jnp.float32), right_factor.T.astype(jnp.float32), precision=highest, preferred_element_type=jnp.float32)
    gram = jnp.dot(left.T.astype(jnp.float32), left.astype(jnp.float32), precision=highest, preferred_element_type=jnp.float32)
    factor = jnp.linalg.cholesky(gram)
    ortho = jax.scipy.linalg.solve_triangular(factor, left.T, lower=True).T
    right_t = jnp.dot(ortho.T.astype(jnp.float32), buffer.astype(jnp.float32), precision=highest, preferred_element_type=jnp.float32)
    scale = jnp.sqrt(lax.optimization_barrier(jnp.sum(right_t * right_t, axis=1)) / N + eps_norm)
    new_right = right_t / scale[:, None]
    new_momentum = buffer - decay_keep * jnp.dot(ortho.astype(jnp.float32), right_t.astype(jnp.float32), precision=highest, preferred_element_type=jnp.float32)
    new_weights = weights - step_size * jnp.dot(ortho.astype(jnp.float32), new_right.astype(jnp.float32), precision=highest, preferred_element_type=jnp.float32)
    return (new_weights, new_momentum, new_right)
```

```python
import jax
import jax.numpy as jnp
from jax import lax
from jax.experimental import pallas as pl
from jax.experimental.pallas import tpu as pltpu
from jax.sharding import Mesh, PartitionSpec as P

N = 28672
R = 512
Z = 8
XY = 16
TILE = 128

decay_keep = 0.05
step_size = 0.5
eps_norm = 1e-06

F32 = jnp.float32
HIGHEST = lax.Precision.HIGHEST


def split_three(values):
    high = values.astype(jnp.bfloat16).astype(F32)
    rest = values - high
    middle = rest.astype(jnp.bfloat16).astype(F32)
    low = (rest - middle).astype(jnp.bfloat16).astype(F32)
    return high, middle, low


def inverse_root(value):
    guess = lax.rsqrt(value)
    return guess * (1.5 - 0.5 * value * (guess * guess))


def invert_factor_8(entries):
    size = len(entries)
    left = [row[:] for row in entries]
    inverse = [[None] * size for _ in range(size)]
    for j in range(size):
        root = inverse_root(left[j][j])
        column = [None] * size
        for i in range(j + 1, size):
            column[i] = left[i][j] * root
        for i in range(j + 1, size):
            for k in range(j + 1, i + 1):
                left[i][k] = left[i][k] - column[i] * column[k]
        for c in range(j):
            inverse[j][c] = inverse[j][c] * root
        inverse[j][j] = root
        for i in range(j + 1, size):
            for c in range(j + 1):
                term = column[i] * inverse[j][c]
                inverse[i][c] = -term if inverse[i][c] is None else inverse[i][c] - term
    return inverse


def invert_factor_tile(state, result):
    sublane = lax.broadcasted_iota(jnp.int32, (8, TILE), 0)
    for step in range(TILE // 8):
        at = 8 * step
        rows = state[at : at + 8, :]
        lanes = [jnp.broadcast_to(rows[:, at + j : at + j + 1], (8, TILE)) for j in range(8)]
        entries = [
            [jnp.broadcast_to(lanes[j][i : i + 1, :], (8, TILE)) for j in range(i + 1)] for i in range(8)
        ]
        inverse = invert_factor_8(entries)
        first, second = None, None
        for j in range(8):
            column = jnp.zeros((8, TILE), F32)
            for i in range(j, 8):
                column = jnp.where(sublane == i, inverse[i][j], column)
            one = column * jnp.broadcast_to(rows[j : j + 1, :TILE], (8, TILE))
            two = column * jnp.broadcast_to(rows[j : j + 1, TILE:], (8, TILE))
            first = one if first is None else first + one
            second = two if second is None else second + two
        result[at : at + 8, :] = second
        if at + 8 < TILE:
            high, middle, low = split_three(jnp.concatenate([first, second], 1))
            right = jnp.concatenate([high, middle, high, low, high, middle], 0).astype(jnp.bfloat16)
            high, middle, low = high[:, :TILE], middle[:, :TILE], low[:, :TILE]
            left = jnp.concatenate([high, high, middle, high, low, middle], 0).astype(jnp.bfloat16)
            update = lax.dot_general(left, right, (((0,), (0,)), ((), ())), preferred_element_type=F32)
            state[at + 8 :, :] = state[at + 8 :, :] - update[at + 8 :, :]


def inverse_factor_kernel(first, last, rest_in, inverse_in, result_in, rest, inverse, result, state, tile, panel):
    identity = jnp.where(
        lax.broadcasted_iota(jnp.int32, (TILE, TILE), 0) == lax.broadcasted_iota(jnp.int32, (TILE, TILE), 1), 1.0, 0.0
    )
    rest[...] = rest_in[...]
    if first == 0:
        rows = lax.broadcasted_iota(jnp.int32, (R, R), 0)
        columns = lax.broadcasted_iota(jnp.int32, (R, R), 1)
        inverse[...] = jnp.where(rows == columns, 1.0, 0.0)
    else:
        inverse[...] = inverse_in[...]
        result[...] = result_in[...]

    @pl.loop(first, last)
    def _(k):
        at = pl.multiple_of(k * TILE, TILE)
        state[:, :TILE] = rest[pl.ds(at, TILE), pl.ds(at, TILE)]
        state[:, TILE:] = identity
        invert_factor_tile(state, tile)
        upper = jnp.dot(tile[...], rest[pl.ds(at, TILE), :], precision=HIGHEST, preferred_element_type=F32)
        lower = jnp.dot(tile[...], inverse[pl.ds(at, TILE), :], precision=HIGHEST, preferred_element_type=F32)
        result[pl.ds(at, TILE), :] = lower
        panel[...] = upper
        for i in range(1, R // TILE):

            @pl.when(i > k)
            def _():
                below = pl.ds(i * TILE, TILE)
                factor = panel[:, i * TILE : (i + 1) * TILE]
                dims = (((0,), (0,)), ((), ()))
                rest[below, :] -= lax.dot_general(factor, upper, dims, precision=HIGHEST, preferred_element_type=F32)
                inverse[below, :] -= lax.dot_general(factor, lower, dims, precision=HIGHEST, preferred_element_type=F32)


def factor_steps(first, last, rest, inverse=None, result=None):
    whole = pl.BlockSpec(memory_space=pltpu.VMEM)
    square = jax.ShapeDtypeStruct((R, R), F32)
    given = (rest,) if first == 0 else (rest, inverse, result)

    def kernel(*refs):
        if first == 0:
            inverse_factor_kernel(first, last, refs[0], None, None, *refs[1:])
        else:
            inverse_factor_kernel(first, last, *refs)

    return pl.pallas_call(
        kernel,
        out_shape=(square, square, square),
        in_specs=[whole] * len(given),
        out_specs=(whole, whole, whole),
        scratch_shapes=[pltpu.VMEM((TILE, 2 * TILE), F32), pltpu.VMEM((TILE, TILE), F32), pltpu.VMEM((TILE, R), F32)],
        compiler_params=pltpu.CompilerParams(vmem_limit_bytes=24 * 2**20),
        cost_estimate=pl.CostEstimate(flops=10**10, bytes_accessed=2 * 4 * R * R, transcendentals=R),
        name="inverse_factor",
    )(*given)


def split_two(values):
    high = values.astype(jnp.bfloat16)
    return high, (values - high.astype(F32)).astype(jnp.bfloat16)


def product3(first, second, dims):
    def one(a, b):
        return lax.dot_general(a, b, (dims, ((), ())), preferred_element_type=F32)

    return one(first[0], second[0]) + (one(first[0], second[1]) + one(first[1], second[0]))


WIDTH = 256
NN = ((1,), (0,))
NT = ((1,), (1,))
LIMIT = 32 * 2**20


def call(kernel, steps, operands, specs, outs, out_specs, scratch=(), name=None, flops=10**9):
    return pl.pallas_call(
        kernel,
        grid=(steps,),
        out_shape=outs,
        in_specs=specs,
        out_specs=out_specs,
        scratch_shapes=list(scratch),
        compiler_params=pltpu.CompilerParams(vmem_limit_bytes=LIMIT, dimension_semantics=("arbitrary",)),
        cost_estimate=pl.CostEstimate(flops=flops, bytes_accessed=4 * 2**20, transcendentals=0),
        name=name,
    )(*operands)


def wide(rows):
    return pl.BlockSpec((rows, WIDTH), lambda j: (0, j))


def whole(*shape):
    return pl.BlockSpec(shape, lambda j: (0,) * len(shape))


def left_product(blocks, chip):
    rows, columns = chip.shape
    ranks = sum(b.shape[0] for b in blocks)

    def kernel(*refs):
        parts, chip_ref, out = refs[:-2], refs[-2], refs[-1]
        right = jnp.concatenate([p[...] for p in parts], 0)
        term = product3(split_two(right), split_two(chip_ref[...]), NT)

        @pl.when(pl.program_id(0) == 0)
        def _():
            out[...] = term

        @pl.when(pl.program_id(0) > 0)
        def _():
            out[...] += term

    return call(
        kernel,
        columns // WIDTH,
        (*blocks, chip),
        [wide(b.shape[0]) for b in blocks] + [wide(rows)],
        jax.ShapeDtypeStruct((ranks, rows), F32),
        whole(ranks, rows),
        name="left_product",
    )


def right_product(left, chip):
    ranks, rows = left.shape
    columns = chip.shape[1]

    def kernel(left_ref, chip_ref, out, high, low):
        @pl.when(pl.program_id(0) == 0)
        def _():
            high[...], low[...] = split_two(left_ref[...])

        out[...] = product3((high[...], low[...]), split_two(chip_ref[...]), NN)

    half = pltpu.VMEM((ranks, rows), jnp.bfloat16)
    return call(
        kernel,
        columns // WIDTH,
        (left, chip),
        [whole(ranks, rows), wide(rows)],
        jax.ShapeDtypeStruct((ranks, columns), F32),
        wide(ranks),
        (half, half),
        name="right_product",
    )


def right_and_squares(inverse, product):
    columns = product.shape[1]
    steps = columns // WIDTH

    def kernel(inverse_ref, product_ref, out, sums, high, low, total):
        j = pl.program_id(0)

        @pl.when(j == 0)
        def _():
            high[...], low[...] = split_two(inverse_ref[...])
            total[...] = jnp.zeros_like(total)

        right = product3((high[...], low[...]), split_two(product_ref[...]), NN)
        out[...] = right
        squares = right * right
        total[...] += squares[:, :128] + squares[:, 128:]

        @pl.when(j == steps - 1)
        def _():
            sums[...] = lax.dot_general(
                jnp.ones((8, 128), F32), total[...], (NT, ((), ())), precision=HIGHEST, preferred_element_type=F32
            )

    half = pltpu.VMEM((R, R), jnp.bfloat16)
    return call(
        kernel,
        steps,
        (inverse, product),
        [whole(R, R), wide(R)],
        (jax.ShapeDtypeStruct((R, columns), F32), jax.ShapeDtypeStruct((8, R), F32)),
        (wide(R), whole(8, R)),
        (half, half, pltpu.VMEM((R, 128), F32)),
        name="right_and_squares",
    )


def momentum_update(buffer, ortho, right):
    rows, columns = buffer.shape

    def kernel(buffer_ref, ortho_ref, right_ref, out, high, low):
        @pl.when(pl.program_id(0) == 0)
        def _():
            high[...], low[...] = split_two(ortho_ref[...])

        out[...] = buffer_ref[...] - decay_keep * product3((high[...], low[...]), split_two(right_ref[...]), NN)

    half = pltpu.VMEM((rows, R), jnp.bfloat16)
    return call(
        kernel,
        columns // WIDTH,
        (buffer, ortho, right),
        [wide(rows), whole(rows, R), wide(R)],
        jax.ShapeDtypeStruct((rows, columns), F32),
        wide(rows),
        (half, half),
        name="momentum_update",
    )


def weights_update(weights, ortho, right, sums, start, share):
    rows, columns = weights.shape
    count = sums.shape[0]

    def kernel(start_ref, weights_ref, ortho_ref, right_ref, sums_ref, out, own, high, low, own_scale):
        at = pl.multiple_of(start_ref[0], share)

        @pl.when(pl.program_id(0) == 0)
        def _():
            scale = jnp.sqrt(jnp.sum(sums_ref[...], axis=0, keepdims=True) / N + eps_norm)
            high[...], low[...] = split_two(ortho_ref[...] / scale)
            lanes = lax.broadcasted_iota(jnp.int32, (share, R), 1)
            chosen = lanes == at + lax.broadcasted_iota(jnp.int32, (share, R), 0)
            picked = jnp.sum(jnp.where(chosen, jnp.broadcast_to(scale, (share, R)), 0.0), axis=1, keepdims=True)
            own_scale[...] = jnp.broadcast_to(picked, own_scale.shape)

        out[...] = weights_ref[...] - step_size * product3((high[...], low[...]), split_two(right_ref[...]), NN)
        own[...] = right_ref[pl.ds(at, share), :] / own_scale[...]

    half = pltpu.VMEM((rows, R), jnp.bfloat16)
    return call(
        kernel,
        columns // WIDTH,
        (start, weights, ortho, right, sums),
        [pl.BlockSpec(memory_space=pltpu.SMEM), wide(rows), whole(rows, R), wide(R), whole(count, R)],
        (jax.ShapeDtypeStruct((rows, columns), F32), jax.ShapeDtypeStruct((share, columns), F32)),
        (wide(rows), wide(share)),
        (half, half, pltpu.VMEM((share, WIDTH), F32)),
        name="weights_update",
    )


SIZES = {"z": Z, "core": 2, "x": 4, "y": 4}


def shift(values, axis, by):
    size = SIZES[axis]
    return lax.ppermute(values, axis, [(i, (i + by) % size) for i in range(size)])


def spread(values, axes, count):
    whole = jnp.broadcast_to(values[None], (count,) + values.shape)
    return lax.all_to_all(whole, axes, 0, 0, tiled=True)


def gather_z(own):
    half = own.shape[0] // 2
    below1, above1 = shift(own, "z", 1), shift(own, "z", -1)
    below2, above2 = shift(own, "z", 2), shift(own, "z", -2)
    below3, above3 = shift(below2, "z", 1), shift(above2, "z", -1)
    across = (shift(below3[:half], "z", 1), shift(above3[half:], "z", -1))
    return [own, above1, above2, above3, across, below3, below2, below1]


def dot(first, second, dims, precision):
    return lax.dot_general(
        first, second, ((dims[0], dims[1]), ((), ())), precision=precision, preferred_element_type=F32
    )


def local(weights, momentum, gradient, right_factor):
    core = lax.axis_index("core")
    plane = lax.axis_index("x") * 4 + lax.axis_index("y")
    z = lax.axis_index("z")
    share = right_factor.shape[0]

    buffer = momentum + gradient.astype(F32)
    right = gather_z(right_factor)
    beside = shift(buffer, "core", 1)
    chip = jnp.where(
        core == 0, jnp.concatenate([buffer, beside], 0), jnp.concatenate([beside, buffer], 0)
    )

    blocks = [*right[:4], *right[4], *right[5:]]
    part = left_product(blocks, chip)
    rows = part.shape[1]
    pieces = lax.all_to_all(part.reshape(XY, -1, rows), ("x", "y"), 0, 0, tiled=True)
    left = spread(jnp.sum(pieces, 0), ("x", "y"), XY).reshape(Z, share, rows)
    own = lax.dynamic_slice_in_dim(jnp.concatenate([left, left], 0), (Z - z) % Z, Z, 0)

    product = right_product(own.reshape(Z * share, rows), chip)
    product = lax.psum_scatter(product, "z", scatter_dimension=0, tiled=True)

    other = shift(own, "core", 1)
    left_all = jnp.stack([jnp.where(core == 0, own, other), jnp.where(core == 0, other, own)], 1)
    left_all = left_all.reshape(R, rows)
    height = R // (2 * XY)
    mine = lax.dynamic_slice_in_dim(left_all, (core * XY + plane) * height, height, 0)
    gram = jnp.sum(spread(dot(mine, left_all, ((1,), (1,)), HIGHEST), "z", Z), 0)
    gram = spread(gram, ("x", "y"), XY).reshape(R // 2, R)
    gram_other = shift(gram, "core", 1)
    gram = jnp.where(
        core == 0, jnp.concatenate([gram, gram_other], 0), jnp.concatenate([gram_other, gram], 0)
    )
    state = factor_steps(0, 2, gram)
    state, product = lax.optimization_barrier((state, product))
    product = lax.all_gather(product, ("z", "core"), axis=0, tiled=True)
    _, _, inverse = factor_steps(2, 4, *state)

    height = rows // 2
    left_own = jnp.where(core == 0, left_all[:, :height], left_all[:, height:])
    ortho = dot(left_own, inverse, ((0,), (1,)), HIGHEST)
    right_t, sums = right_and_squares(inverse, product)
    sums = spread(sums[:1], ("x", "y"), XY).reshape(XY, R)
    start = jnp.full((1,), (2 * z + core) * share, jnp.int32)
    new_momentum = momentum_update(buffer, ortho, right_t)
    new_weights, new_right = weights_update(weights, ortho, right_t, sums, start, share)
    return (new_weights, new_momentum, new_right)


def solution(mesh):
    fine = Mesh(mesh.devices.reshape(Z, 2, 4, 4), ("z", "core", "x", "y"))
    spec = P(("z", "core"), ("x", "y"))
    return jax.shard_map(
        local, mesh=fine, in_specs=(spec, spec, spec, spec), out_specs=(spec, spec, spec), check_vma=False
    )
```

```python
import jax
import jax.numpy as jnp
from jax import lax
from jax.experimental import pallas as pl
from jax.experimental.pallas import tpu as pltpu
from jax.sharding import Mesh, PartitionSpec as P

N = 28672
R = 512
Z = 8
XY = 16
TILE = 128

decay_keep = 0.05
step_size = 0.5
eps_norm = 1e-06

F32 = jnp.float32
HIGHEST = lax.Precision.HIGHEST


def split_three(values):
    high = values.astype(jnp.bfloat16).astype(F32)
    rest = values - high
    middle = rest.astype(jnp.bfloat16).astype(F32)
    low = (rest - middle).astype(jnp.bfloat16).astype(F32)
    return high, middle, low


def inverse_root(value):
    guess = lax.rsqrt(value)
    return guess * (1.5 - 0.5 * value * (guess * guess))


def invert_factor_8(entries):
    size = len(entries)
    left = [row[:] for row in entries]
    inverse = [[None] * size for _ in range(size)]
    for j in range(size):
        root = inverse_root(left[j][j])
        column = [None] * size
        for i in range(j + 1, size):
            column[i] = left[i][j] * root
        for i in range(j + 1, size):
            for k in range(j + 1, i + 1):
                left[i][k] = left[i][k] - column[i] * column[k]
        for c in range(j):
            inverse[j][c] = inverse[j][c] * root
        inverse[j][j] = root
        for i in range(j + 1, size):
            for c in range(j + 1):
                term = column[i] * inverse[j][c]
                inverse[i][c] = -term if inverse[i][c] is None else inverse[i][c] - term
    return inverse


def invert_factor_tile(state, result):
    sublane = lax.broadcasted_iota(jnp.int32, (8, TILE), 0)
    for step in range(TILE // 8):
        at = 8 * step
        rows = state[at : at + 8, :]
        lanes = [jnp.broadcast_to(rows[:, at + j : at + j + 1], (8, TILE)) for j in range(8)]
        entries = [
            [jnp.broadcast_to(lanes[j][i : i + 1, :], (8, TILE)) for j in range(i + 1)] for i in range(8)
        ]
        inverse = invert_factor_8(entries)
        first, second = None, None
        for j in range(8):
            column = jnp.zeros((8, TILE), F32)
            for i in range(j, 8):
                column = jnp.where(sublane == i, inverse[i][j], column)
            one = column * jnp.broadcast_to(rows[j : j + 1, :TILE], (8, TILE))
            two = column * jnp.broadcast_to(rows[j : j + 1, TILE:], (8, TILE))
            first = one if first is None else first + one
            second = two if second is None else second + two
        result[at : at + 8, :] = second
        if at + 8 < TILE:
            high, middle, low = split_three(jnp.concatenate([first, second], 1))
            right = jnp.concatenate([high, middle, high, low, high, middle], 0).astype(jnp.bfloat16)
            high, middle, low = high[:, :TILE], middle[:, :TILE], low[:, :TILE]
            left = jnp.concatenate([high, high, middle, high, low, middle], 0).astype(jnp.bfloat16)
            update = lax.dot_general(left, right, (((0,), (0,)), ((), ())), preferred_element_type=F32)
            state[at + 8 :, :] = state[at + 8 :, :] - update[at + 8 :, :]


def inverse_factor_kernel(first, last, rest_in, inverse_in, rest, inverse, state, tile, panel):
    identity = jnp.where(
        lax.broadcasted_iota(jnp.int32, (TILE, TILE), 0) == lax.broadcasted_iota(jnp.int32, (TILE, TILE), 1), 1.0, 0.0
    )
    rest[...] = rest_in[...]
    if first == 0:
        rows = lax.broadcasted_iota(jnp.int32, (R, R), 0)
        columns = lax.broadcasted_iota(jnp.int32, (R, R), 1)
        inverse[...] = jnp.where(rows == columns, 1.0, 0.0)
    else:
        inverse[...] = inverse_in[...]

    @pl.loop(first, last)
    def _(k):
        at = pl.multiple_of(k * TILE, TILE)
        state[:, :TILE] = rest[pl.ds(at, TILE), pl.ds(at, TILE)]
        state[:, TILE:] = identity
        invert_factor_tile(state, tile)
        upper = jnp.dot(tile[...], rest[pl.ds(at, TILE), :], precision=HIGHEST, preferred_element_type=F32)
        lower = jnp.dot(tile[...], inverse[pl.ds(at, TILE), :], precision=HIGHEST, preferred_element_type=F32)
        inverse[pl.ds(at, TILE), :] = lower
        panel[...] = upper
        for i in range(1, R // TILE):

            @pl.when(i > k)
            def _():
                below = pl.ds(i * TILE, TILE)
                factor = panel[:, i * TILE : (i + 1) * TILE]
                dims = (((0,), (0,)), ((), ()))
                rest[below, :] -= lax.dot_general(factor, upper, dims, precision=HIGHEST, preferred_element_type=F32)
                inverse[below, :] -= lax.dot_general(factor, lower, dims, precision=HIGHEST, preferred_element_type=F32)


def factor_steps(first, last, given, earlier=()):
    whole = pl.BlockSpec(memory_space=pltpu.VMEM)
    square = jax.ShapeDtypeStruct((R, R), F32)
    count = len(given)

    def kernel(*refs):
        inverse_in = refs[1] if count > 1 else None
        inverse_factor_kernel(first, last, refs[0], inverse_in, *refs[count + len(earlier) :])

    return pl.pallas_call(
        kernel,
        out_shape=(square, square),
        in_specs=[whole] * count + [pl.BlockSpec(memory_space=pl.ANY)] * len(earlier),
        out_specs=(whole, whole),
        scratch_shapes=[pltpu.VMEM((TILE, 2 * TILE), F32), pltpu.VMEM((TILE, TILE), F32), pltpu.VMEM((TILE, R), F32)],
        compiler_params=pltpu.CompilerParams(vmem_limit_bytes=12 * 2**20),
        cost_estimate=pl.CostEstimate(flops=8 * 10**9 * (last - first), bytes_accessed=2 * 4 * R * R, transcendentals=R),
        name="inverse_factor",
    )(*given, *earlier)


def split_two(values):
    high = values.astype(jnp.bfloat16)
    return high, (values - high.astype(F32)).astype(jnp.bfloat16)


def product3(first, second, dims):
    def one(a, b):
        return lax.dot_general(a, b, (dims, ((), ())), preferred_element_type=F32)

    return one(first[0], second[0]) + (one(first[0], second[1]) + one(first[1], second[0]))


WIDTH = 896
NN = ((1,), (0,))
NT = ((1,), (1,))
LIMIT = 20 * 2**20


def call(kernel, steps, operands, specs, outs, out_specs, scratch=(), name=None, flops=3 * 10**9, limit=LIMIT):
    return pl.pallas_call(
        kernel,
        grid=(steps,),
        out_shape=outs,
        in_specs=specs,
        out_specs=out_specs,
        scratch_shapes=list(scratch),
        compiler_params=pltpu.CompilerParams(vmem_limit_bytes=limit, dimension_semantics=("arbitrary",)),
        cost_estimate=pl.CostEstimate(flops=flops, bytes_accessed=4 * 2**20, transcendentals=0),
        name=name,
    )(*operands)


def wide(rows):
    return pl.BlockSpec((rows, WIDTH), lambda j: (0, j))


def whole(*shape):
    return pl.BlockSpec(shape, lambda j: (0,) * len(shape))


def left_product(blocks, chip):
    rows, columns = chip.shape
    ranks = sum(b.shape[0] for b in blocks)

    def kernel(*refs):
        parts, chip_ref, out = refs[:-2], refs[-2], refs[-1]
        right = jnp.concatenate([p[...] for p in parts], 0)
        term = product3(split_two(right), split_two(chip_ref[...]), NT)

        @pl.when(pl.program_id(0) == 0)
        def _():
            out[...] = term

        @pl.when(pl.program_id(0) > 0)
        def _():
            out[...] += term

    return call(
        kernel,
        columns // WIDTH,
        (*blocks, chip),
        [wide(b.shape[0]) for b in blocks] + [wide(rows)],
        jax.ShapeDtypeStruct((ranks, rows), F32),
        whole(ranks, rows),
        name="left_product",
    )


def right_product(left, chip):
    ranks, rows = left.shape
    columns = chip.shape[1]

    def kernel(left_ref, chip_ref, out, high, low):
        @pl.when(pl.program_id(0) == 0)
        def _():
            high[...], low[...] = split_two(left_ref[...])

        out[...] = product3((high[...], low[...]), split_two(chip_ref[...]), NN)

    half = pltpu.VMEM((ranks, rows), jnp.bfloat16)
    return call(
        kernel,
        columns // WIDTH,
        (left, chip),
        [whole(ranks, rows), wide(rows)],
        jax.ShapeDtypeStruct((ranks, columns), F32),
        wide(ranks),
        (half, half),
        name="right_product",
    )


def right_and_squares(inverse, pieces, place):
    columns = pieces[0][0].shape[1]
    share = R // (2 * Z)
    steps = columns // WIDTH
    count = len(pieces)

    def kernel(place_ref, inverse_ref, *refs):
        parts, (out, sums, high, low, total, high_product, low_product) = refs[:count], refs[count:]
        j = pl.program_id(0)

        @pl.when(j == 0)
        def _():
            high[...], low[...] = split_two(inverse_ref[...])
            total[...] = jnp.zeros_like(total)

        for part, (_, chip, core, row) in zip(parts, pieces):
            block = lax.rem(place_ref[0] + chip, Z) * 2 + (place_ref[1] + core) % 2
            rows = pl.ds(pl.multiple_of(block * share + row, 16), part.shape[0])
            high_product[rows, :], low_product[rows, :] = split_two(part[...])
        right = product3((high[...], low[...]), (high_product[...], low_product[...]), NN)
        out[...] = right
        squares = right * right
        total[...] += sum(squares[:, i : i + 128] for i in range(0, WIDTH, 128))

        @pl.when(j == steps - 1)
        def _():
            sums[...] = lax.dot_general(
                jnp.ones((8, 128), F32), total[...], (NT, ((), ())), precision=HIGHEST, preferred_element_type=F32
            )

    half = pltpu.VMEM((R, R), jnp.bfloat16)
    half_product = pltpu.VMEM((R, WIDTH), jnp.bfloat16)
    return call(
        kernel,
        steps,
        (place, inverse, *(p[0] for p in pieces)),
        [pl.BlockSpec(memory_space=pltpu.SMEM), whole(R, R)] + [wide(p[0].shape[0]) for p in pieces],
        (jax.ShapeDtypeStruct((R, columns), F32), jax.ShapeDtypeStruct((8, R), F32)),
        (wide(R), whole(8, R)),
        (half, half, pltpu.VMEM((R, 128), F32), half_product, half_product),
        name="right_and_squares",
        limit=32 * 2**20,
    )


def momentum_update(buffer, ortho, right):
    rows, columns = buffer.shape

    def kernel(buffer_ref, ortho_ref, right_ref, out, high, low):
        @pl.when(pl.program_id(0) == 0)
        def _():
            high[...], low[...] = split_two(ortho_ref[...])

        out[...] = buffer_ref[...] - decay_keep * product3((high[...], low[...]), split_two(right_ref[...]), NN)

    half = pltpu.VMEM((rows, R), jnp.bfloat16)
    return call(
        kernel,
        columns // WIDTH,
        (buffer, ortho, right),
        [wide(rows), whole(rows, R), wide(R)],
        jax.ShapeDtypeStruct((rows, columns), F32),
        wide(rows),
        (half, half),
        name="momentum_update",
        limit=40 * 2**20,
    )


def weights_update(weights, ortho, right, sums, start, share):
    rows, columns = weights.shape
    count = sums.shape[0]

    def kernel(start_ref, weights_ref, ortho_ref, right_ref, sums_ref, out, own, high, low, own_scale):
        at = pl.multiple_of(start_ref[0], share)

        @pl.when(pl.program_id(0) == 0)
        def _():
            scale = jnp.sqrt(jnp.sum(sums_ref[...], axis=0, keepdims=True) / N + eps_norm)
            high[...], low[...] = split_two(ortho_ref[...] / scale)
            lanes = lax.broadcasted_iota(jnp.int32, (share, R), 1)
            chosen = lanes == at + lax.broadcasted_iota(jnp.int32, (share, R), 0)
            picked = jnp.sum(jnp.where(chosen, jnp.broadcast_to(scale, (share, R)), 0.0), axis=1, keepdims=True)
            own_scale[...] = jnp.broadcast_to(picked, own_scale.shape)

        out[...] = weights_ref[...] - step_size * product3((high[...], low[...]), split_two(right_ref[...]), NN)
        own[...] = right_ref[pl.ds(at, share), :] / own_scale[...]

    half = pltpu.VMEM((rows, R), jnp.bfloat16)
    return call(
        kernel,
        columns // WIDTH,
        (start, weights, ortho, right, sums),
        [pl.BlockSpec(memory_space=pltpu.SMEM), wide(rows), whole(rows, R), wide(R), whole(count, R)],
        (jax.ShapeDtypeStruct((rows, columns), F32), jax.ShapeDtypeStruct((share, columns), F32)),
        (wide(rows), wide(share)),
        (half, half, pltpu.VMEM((share, WIDTH), F32)),
        name="weights_update",
        limit=40 * 2**20,
    )


SIZES = {"z": Z, "core": 2, "x": 4, "y": 4}


def shift(values, axis, by):
    size = SIZES[axis]
    return lax.ppermute(values, axis, [(i, (i + by) % size) for i in range(size)])


def spread(values, axes, count):
    whole = jnp.broadcast_to(values[None], (count,) + values.shape)
    return lax.all_to_all(whole, axes, 0, 0, tiled=True)


def gather_z(own):
    half = own.shape[0] // 2
    below1, above1 = shift(own, "z", 1), shift(own, "z", -1)
    below2, above2 = shift(own, "z", 2), shift(own, "z", -2)
    below3, above3 = shift(below2, "z", 1), shift(above2, "z", -1)
    across = (shift(below3[:half], "z", 1), shift(above3[half:], "z", -1))
    return [own, above1, above2, above3, across, below3, below2, below1]


def after(values, earlier):
    first = earlier[(0,) * earlier.ndim]
    return jnp.where(first == first, values, first)


def scatter_z(parts, then):
    share = parts.shape[0] // Z
    half = share // 2
    up, down = shift(parts[: 2 * share], "z", 1), shift(parts[2 * share : 4 * share], "z", -1)
    top = shift(parts[4 * share : 4 * share + half], "z", 2)
    bottom = shift(parts[4 * share + half : 5 * share], "z", -2)
    ahead = parts[5 * share : 6 * share] + up[share:] + jnp.pad(top, ((0, half), (0, 0)))
    behind = parts[6 * share : 7 * share] + down[share:] + jnp.pad(bottom, ((half, 0), (0, 0)))
    ahead, behind = after(ahead, then), after(behind, then)
    up2, down2 = shift(ahead, "z", 2), shift(behind, "z", -2)
    return parts[7 * share :] + up[:share] + down[:share] + up2 + down2, after(after(then, ahead), behind)


def dot(first, second, dims, precision):
    return lax.dot_general(
        first, second, ((dims[0], dims[1]), ((), ())), precision=precision, preferred_element_type=F32
    )


SENT = (1, 3, 7, 5, 4, 2, 6, 0)


def local(weights, momentum, gradient, right_factor):
    core = lax.axis_index("core")
    plane = lax.axis_index("x") * 4 + lax.axis_index("y")
    z = lax.axis_index("z")
    share = right_factor.shape[0]
    half = share // 2

    buffer = momentum + gradient.astype(F32)
    right = gather_z(right_factor)
    beside = shift(buffer, "core", 1)
    chip = jnp.where(
        core == 0, jnp.concatenate([buffer, beside], 0), jnp.concatenate([beside, buffer], 0)
    )

    blocks = [right[k] for k in SENT]
    blocks = [*blocks[:4], *blocks[4], *blocks[5:]]
    part = left_product(blocks, chip)
    rows = part.shape[1]
    pieces = lax.all_to_all(part.reshape(XY, -1, rows), ("x", "y"), 0, 0, tiled=True)
    left = spread(jnp.sum(pieces, 0), ("x", "y"), XY).reshape(Z, share, rows)

    product = right_product(left.reshape(Z * share, rows), chip)

    in_turn = [left[SENT.index(k)] for k in range(Z)]
    own = lax.dynamic_slice_in_dim(jnp.stack(in_turn + in_turn), (Z - z) % Z, Z, 0)
    other = shift(own, "core", 1)
    left_all = jnp.stack([jnp.where(core == 0, own, other), jnp.where(core == 0, other, own)], 1)
    left_all = left_all.reshape(R, rows)
    height = R // (2 * XY)
    mine = lax.dynamic_slice_in_dim(left_all, (core * XY + plane) * height, height, 0)
    gram = jnp.sum(spread(dot(mine, left_all, ((1,), (1,)), HIGHEST), "z", Z), 0)
    product, gram = scatter_z(product, gram)
    gram = spread(gram, ("x", "y"), XY).reshape(R // 2, R)
    gram_other = shift(gram, "core", 1)
    gram = jnp.where(
        core == 0, jnp.concatenate([gram, gram_other], 0), jnp.concatenate([gram_other, gram], 0)
    )

    product = after(product, gram)
    below2, above2 = shift(product, "z", 2), shift(product, "z", -2)
    state = factor_steps(0, 1, (gram,))
    below = shift(after(jnp.concatenate([product, below2], 0), state[0]), "z", 1)
    above = shift(after(jnp.concatenate([product, above2], 0), state[0]), "z", -1)
    top, bottom = shift(after(below2[:half], state[0]), "z", 2), shift(after(above2[half:], state[0]), "z", -2)
    state = factor_steps(1, 3, state, (below2, above2))
    pieces = [(product, 0, 0), (below2, 6, 0), (above2, 2, 0), (top, 4, 0), (bottom, 4, half)]
    pieces += [(below[:share], 7, 0), (below[share:], 5, 0), (above[:share], 1, 0), (above[share:], 3, 0)]
    pieces = [(v, k, 0, row) for v, k, row in pieces] + [(shift(v, "core", 1), k, 1, row) for v, k, row in pieces]
    _, inverse = factor_steps(3, 4, state, (below, above, top, bottom))

    height = rows // 2
    left_own = jnp.where(core == 0, left_all[:, :height], left_all[:, height:])
    ortho = dot(left_own, inverse, ((0,), (1,)), HIGHEST)
    right_t, sums = right_and_squares(inverse, pieces, jnp.stack([z, core]).astype(jnp.int32))
    sums = spread(sums[:1], ("x", "y"), XY).reshape(XY, R)
    start = jnp.full((1,), (2 * z + core) * share, jnp.int32)
    new_momentum = momentum_update(buffer, ortho, right_t)
    new_weights, new_right = weights_update(weights, ortho, right_t, sums, start, share)
    return (new_weights, new_momentum, new_right)


def solution(mesh):
    fine = Mesh(mesh.devices.reshape(Z, 2, 4, 4), ("z", "core", "x", "y"))
    spec = P(("z", "core"), ("x", "y"))
    return jax.shard_map(
        local, mesh=fine, in_specs=(spec, spec, spec, spec), out_specs=(spec, spec, spec), check_vma=False
    )
```

```python
import jax
import jax.numpy as jnp
from jax import lax
from jax.experimental import pallas as pl
from jax.experimental.pallas import tpu as pltpu
from jax.sharding import Mesh, PartitionSpec as P

N = 28672
R = 512
Z = 8
XY = 16
TILE = 128

decay_keep = 0.05
step_size = 0.5
eps_norm = 1e-06

F32 = jnp.float32
HIGHEST = lax.Precision.HIGHEST


def split_three(values):
    high = values.astype(jnp.bfloat16).astype(F32)
    rest = values - high
    middle = rest.astype(jnp.bfloat16).astype(F32)
    low = (rest - middle).astype(jnp.bfloat16).astype(F32)
    return high, middle, low


def invert_factor_8(entries):
    size = len(entries)
    left = [row[:] for row in entries]
    inverse = [[None] * size for _ in range(size)]
    for j in range(size):
        root = lax.rsqrt(left[j][j])
        square = root * root
        for i in range(j + 1, size):
            share = left[i][j] * square
            for k in range(j + 1, i + 1):
                left[i][k] = left[i][k] - share * left[k][j]
        column = [None] * size
        for i in range(j + 1, size):
            column[i] = left[i][j] * root
        for c in range(j):
            inverse[j][c] = inverse[j][c] * root
        inverse[j][j] = root
        for i in range(j + 1, size):
            for c in range(j + 1):
                term = column[i] * inverse[j][c]
                inverse[i][c] = -term if inverse[i][c] is None else inverse[i][c] - term
    return inverse


def invert_factor_tile(state, result):
    sublane = lax.broadcasted_iota(jnp.int32, (8, TILE), 0)
    lane = lax.broadcasted_iota(jnp.int32, (8, TILE), 1)
    rows = state[0:8, :]
    for step in range(TILE // 8):
        at = 8 * step
        lanes = [jnp.broadcast_to(rows[:, at + j : at + j + 1], (8, TILE)) for j in range(8)]
        entries = [
            [jnp.broadcast_to(lanes[j][i : i + 1, :], (8, TILE)) for j in range(i + 1)] for i in range(8)
        ]
        inverse = invert_factor_8(entries)
        first, second = None, None
        for j in range(8):
            column = jnp.zeros((8, TILE), F32)
            for i in range(j, 8):
                column = jnp.where(sublane == i, inverse[i][j], column)
            one = column * jnp.broadcast_to(rows[j : j + 1, :TILE], (8, TILE))
            two = column * jnp.broadcast_to(rows[j : j + 1, TILE:], (8, TILE))
            first = one if first is None else first + one
            second = two if second is None else second + two
        result[at : at + 8, :] = second
        after = at + 8
        if after == TILE:
            break
        next_first, next_second = state[after : after + 8, :TILE], state[after : after + 8, TILE:]
        for k in range(8):
            one = jnp.broadcast_to(first[k : k + 1, :], (8, TILE))
            two = jnp.broadcast_to(second[k : k + 1, :], (8, TILE))
            factor = jnp.sum(jnp.where(lane == after + sublane, one, 0.0), axis=1, keepdims=True)
            next_first, next_second = next_first - factor * one, next_second - factor * two
        rows = jnp.concatenate([next_first, next_second], 1)
        if after + 8 < TILE:
            high, middle, low = split_three(jnp.concatenate([first, second], 1))
            right = jnp.concatenate([high, middle, high, low, high, middle], 0).astype(jnp.bfloat16)
            high, middle, low = high[:, :TILE], middle[:, :TILE], low[:, :TILE]
            left = jnp.concatenate([high, high, middle, high, low, middle], 0).astype(jnp.bfloat16)
            update = lax.dot_general(left, right, (((0,), (0,)), ((), ())), preferred_element_type=F32)
            state[after + 8 :, :] = state[after + 8 :, :] - update[after + 8 :, :]


def inverse_factor_kernel(gram, earlier, inverse, rest, state, tile, panel):
    rows = lax.broadcasted_iota(jnp.int32, (R, R), 0)
    columns = lax.broadcasted_iota(jnp.int32, (R, R), 1)
    rest[...] = gram[...]
    inverse[...] = jnp.where(rows == columns, 1.0, 0.0)
    identity = jnp.where(
        lax.broadcasted_iota(jnp.int32, (TILE, TILE), 0) == lax.broadcasted_iota(jnp.int32, (TILE, TILE), 1), 1.0, 0.0
    )

    @pl.loop(0, R // TILE)
    def _(k):
        at = pl.multiple_of(k * TILE, TILE)
        state[:, :TILE] = rest[pl.ds(at, TILE), pl.ds(at, TILE)]
        state[:, TILE:] = identity
        invert_factor_tile(state, tile)
        upper = jnp.dot(tile[...], rest[pl.ds(at, TILE), :], precision=HIGHEST, preferred_element_type=F32)
        lower = jnp.dot(tile[...], inverse[pl.ds(at, TILE), :], precision=HIGHEST, preferred_element_type=F32)
        inverse[pl.ds(at, TILE), :] = lower
        panel[...] = upper
        for i in range(1, R // TILE):

            @pl.when(i > k)
            def _():
                below = pl.ds(i * TILE, TILE)
                factor = panel[:, i * TILE : (i + 1) * TILE]
                dims = (((0,), (0,)), ((), ()))
                rest[below, :] -= lax.dot_general(factor, upper, dims, precision=HIGHEST, preferred_element_type=F32)
                inverse[below, :] -= lax.dot_general(factor, lower, dims, precision=HIGHEST, preferred_element_type=F32)


def inverse_factor(gram, earlier):
    whole = pl.BlockSpec(memory_space=pltpu.VMEM)
    return pl.pallas_call(
        inverse_factor_kernel,
        out_shape=jax.ShapeDtypeStruct((R, R), F32),
        in_specs=[whole, pl.BlockSpec(memory_space=pl.ANY)],
        out_specs=whole,
        scratch_shapes=[
            pltpu.VMEM((R, R), F32),
            pltpu.VMEM((TILE, 2 * TILE), F32),
            pltpu.VMEM((TILE, TILE), F32),
            pltpu.VMEM((TILE, R), F32),
        ],
        compiler_params=pltpu.CompilerParams(vmem_limit_bytes=12 * 2**20),
        cost_estimate=pl.CostEstimate(flops=3 * 10**10, bytes_accessed=2 * 4 * R * R, transcendentals=R),
        name="inverse_factor",
    )(gram, earlier)


def split_two(values):
    high = values.astype(jnp.bfloat16)
    return high, (values - high.astype(F32)).astype(jnp.bfloat16)


def product3(first, second, dims):
    def one(a, b):
        return lax.dot_general(a, b, (dims, ((), ())), preferred_element_type=F32)

    return one(first[0], second[0]) + (one(first[0], second[1]) + one(first[1], second[0]))


WIDTH = 896
NN = ((1,), (0,))
NT = ((1,), (1,))
LIMIT = 52 * 2**20


def call(kernel, steps, operands, specs, outs, out_specs, scratch=(), name=None, flops=3 * 10**9):
    return pl.pallas_call(
        kernel,
        grid=(steps,),
        out_shape=outs,
        in_specs=specs,
        out_specs=out_specs,
        scratch_shapes=list(scratch),
        compiler_params=pltpu.CompilerParams(vmem_limit_bytes=LIMIT, dimension_semantics=("arbitrary",)),
        cost_estimate=pl.CostEstimate(flops=flops, bytes_accessed=4 * 2**20, transcendentals=0),
        name=name,
    )(*operands)


def wide(rows):
    return pl.BlockSpec((rows, WIDTH), lambda j: (0, j))


def whole(*shape):
    return pl.BlockSpec(shape, lambda j: (0,) * len(shape))


def left_product(blocks, chip):
    rows, columns = chip.shape
    ranks = sum(b.shape[0] for b in blocks)

    def kernel(*refs):
        parts, chip_ref, out = refs[:-2], refs[-2], refs[-1]
        right = jnp.concatenate([p[...] for p in parts], 0)
        term = product3(split_two(right), split_two(chip_ref[...]), NT)

        @pl.when(pl.program_id(0) == 0)
        def _():
            out[...] = term

        @pl.when(pl.program_id(0) > 0)
        def _():
            out[...] += term

    return call(
        kernel,
        columns // WIDTH,
        (*blocks, chip),
        [wide(b.shape[0]) for b in blocks] + [wide(rows)],
        jax.ShapeDtypeStruct((ranks, rows), F32),
        whole(ranks, rows),
        name="left_product",
    )


def right_product(left, chip):
    ranks, rows = left.shape
    columns = chip.shape[1]

    def kernel(left_ref, chip_ref, out, high, low):
        @pl.when(pl.program_id(0) == 0)
        def _():
            high[...], low[...] = split_two(left_ref[...])

        out[...] = product3((high[...], low[...]), split_two(chip_ref[...]), NN)

    half = pltpu.VMEM((ranks, rows), jnp.bfloat16)
    return call(
        kernel,
        columns // WIDTH,
        (left, chip),
        [whole(ranks, rows), wide(rows)],
        jax.ShapeDtypeStruct((ranks, columns), F32),
        wide(ranks),
        (half, half),
        name="right_product",
    )


def right_and_squares(inverse, product):
    columns = product.shape[1]
    steps = columns // WIDTH

    def kernel(inverse_ref, product_ref, out_high, out_low, sums, high, low, total):
        j = pl.program_id(0)

        @pl.when(j == 0)
        def _():
            high[...], low[...] = split_two(inverse_ref[...])
            total[...] = jnp.zeros_like(total)

        right = product3((high[...], low[...]), split_two(product_ref[...]), NN)
        out_high[...], out_low[...] = split_two(right)
        squares = right * right
        total[...] += sum(squares[:, i : i + 128] for i in range(0, WIDTH, 128))

        @pl.when(j == steps - 1)
        def _():
            sums[...] = lax.dot_general(
                jnp.ones((8, 128), F32), total[...], (NT, ((), ())), precision=HIGHEST, preferred_element_type=F32
            )

    half = pltpu.VMEM((R, R), jnp.bfloat16)
    pair = jax.ShapeDtypeStruct((R, columns), jnp.bfloat16)
    return call(
        kernel,
        steps,
        (inverse, product),
        [whole(R, R), wide(R)],
        (pair, pair, jax.ShapeDtypeStruct((8, R), F32)),
        (wide(R), wide(R), whole(8, R)),
        (half, half, pltpu.VMEM((R, 128), F32)),
        name="right_and_squares",
    )


def momentum_update(buffer, ortho, right):
    rows, columns = buffer.shape

    def kernel(buffer_ref, ortho_ref, right_high, right_low, out, high, low):
        @pl.when(pl.program_id(0) == 0)
        def _():
            high[...], low[...] = split_two(ortho_ref[...])

        out[...] = buffer_ref[...] - decay_keep * product3(
            (high[...], low[...]), (right_high[...], right_low[...]), NN
        )

    half = pltpu.VMEM((rows, R), jnp.bfloat16)
    return call(
        kernel,
        columns // WIDTH,
        (buffer, ortho, *right),
        [wide(rows), whole(rows, R), wide(R), wide(R)],
        jax.ShapeDtypeStruct((rows, columns), F32),
        wide(rows),
        (half, half),
        name="momentum_update",
    )


def weights_update(weights, ortho, right, sums, start, share):
    rows, columns = weights.shape
    count = sums.shape[0]

    def kernel(start_ref, weights_ref, ortho_ref, right_high, right_low, sums_ref, out, own, high, low, own_scale):
        at = pl.multiple_of(start_ref[0], share)

        @pl.when(pl.program_id(0) == 0)
        def _():
            scale = jnp.sqrt(jnp.sum(sums_ref[...], axis=0, keepdims=True) / N + eps_norm)
            high[...], low[...] = split_two(ortho_ref[...] / scale)
            lanes = lax.broadcasted_iota(jnp.int32, (share, R), 1)
            chosen = lanes == at + lax.broadcasted_iota(jnp.int32, (share, R), 0)
            picked = jnp.sum(jnp.where(chosen, jnp.broadcast_to(scale, (share, R)), 0.0), axis=1, keepdims=True)
            own_scale[...] = jnp.broadcast_to(picked, own_scale.shape)

        out[...] = weights_ref[...] - step_size * product3(
            (high[...], low[...]), (right_high[...], right_low[...]), NN
        )
        here = pl.ds(at, share)
        own[...] = (right_high[here, :].astype(F32) + right_low[here, :].astype(F32)) / own_scale[...]

    half = pltpu.VMEM((rows, R), jnp.bfloat16)
    return call(
        kernel,
        columns // WIDTH,
        (start, weights, ortho, *right, sums),
        [pl.BlockSpec(memory_space=pltpu.SMEM), wide(rows), whole(rows, R), wide(R), wide(R), whole(count, R)],
        (jax.ShapeDtypeStruct((rows, columns), F32), jax.ShapeDtypeStruct((share, columns), F32)),
        (wide(rows), wide(share)),
        (half, half, pltpu.VMEM((share, WIDTH), F32)),
        name="weights_update",
    )


SIZES = {"z": Z, "core": 2, "x": 4, "y": 4}


def shift(values, axis, by):
    size = SIZES[axis]
    return lax.ppermute(values, axis, [(i, (i + by) % size) for i in range(size)])


def spread(values, axes, count):
    whole = jnp.broadcast_to(values[None], (count,) + values.shape)
    return lax.all_to_all(whole, axes, 0, 0, tiled=True)


def gather_z(own):
    half = own.shape[0] // 2
    below1, above1 = shift(own, "z", 1), shift(own, "z", -1)
    below2, above2 = shift(own, "z", 2), shift(own, "z", -2)
    below3, above3 = shift(below2, "z", 1), shift(above2, "z", -1)
    across = (shift(below3[:half], "z", 1), shift(above3[half:], "z", -1))
    return [own, above1, above2, above3, across, below3, below2, below1]


def dot(first, second, dims, precision):
    return lax.dot_general(
        first, second, ((dims[0], dims[1]), ((), ())), precision=precision, preferred_element_type=F32
    )


def local(weights, momentum, gradient, right_factor):
    core = lax.axis_index("core")
    plane = lax.axis_index("x") * 4 + lax.axis_index("y")
    z = lax.axis_index("z")
    share = right_factor.shape[0]

    buffer = momentum + gradient.astype(F32)
    right = gather_z(right_factor)
    beside = shift(buffer, "core", 1)
    chip = jnp.where(
        core == 0, jnp.concatenate([buffer, beside], 0), jnp.concatenate([beside, buffer], 0)
    )

    blocks = [*right[:4], *right[4], *right[5:]]
    part = left_product(blocks, chip)
    rows = part.shape[1]
    pieces = lax.all_to_all(part.reshape(XY, -1, rows), ("x", "y"), 0, 0, tiled=True)
    left = spread(jnp.sum(pieces, 0), ("x", "y"), XY).reshape(Z, share, rows)
    own = lax.dynamic_slice_in_dim(jnp.concatenate([left, left], 0), (Z - z) % Z, Z, 0)

    product = right_product(own.reshape(Z * share, rows), chip)
    product = lax.psum_scatter(product, "z", scatter_dimension=0, tiled=True)

    other = shift(own, "core", 1)
    left_all = jnp.stack([jnp.where(core == 0, own, other), jnp.where(core == 0, other, own)], 1)
    left_all = left_all.reshape(R, rows)
    height = R // (2 * XY)
    mine = lax.dynamic_slice_in_dim(left_all, (core * XY + plane) * height, height, 0)
    gram = jnp.sum(spread(dot(mine, left_all, ((1,), (1,)), HIGHEST), "z", Z), 0)
    gram = spread(gram, ("x", "y"), XY).reshape(R // 2, R)
    gram_other = shift(gram, "core", 1)
    gram = jnp.where(
        core == 0, jnp.concatenate([gram, gram_other], 0), jnp.concatenate([gram_other, gram], 0)
    )
    inverse = inverse_factor(gram, product)
    product = lax.all_gather(product, ("z", "core"), axis=0, tiled=True)

    height = rows // 2
    left_own = jnp.where(core == 0, left_all[:, :height], left_all[:, height:])
    ortho = dot(left_own, inverse, ((0,), (1,)), HIGHEST)
    *right_t, sums = right_and_squares(inverse, product)
    sums = spread(sums[:1], ("x", "y"), XY).reshape(XY, R)
    start = jnp.full((1,), (2 * z + core) * share, jnp.int32)
    new_momentum = momentum_update(buffer, ortho, right_t)
    new_weights, new_right = weights_update(weights, ortho, right_t, sums, start, share)
    return (new_weights, new_momentum, new_right)


def solution(mesh):
    fine = Mesh(mesh.devices.reshape(Z, 2, 4, 4), ("z", "core", "x", "y"))
    spec = P(("z", "core"), ("x", "y"))
    return jax.shard_map(
        local, mesh=fine, in_specs=(spec, spec, spec, spec), out_specs=(spec, spec, spec), check_vma=False
    )
```

```python
import jax
import jax.numpy as jnp
from jax import lax
from jax.experimental import pallas as pl
from jax.experimental.pallas import tpu as pltpu
from jax.sharding import Mesh, PartitionSpec as P

N = 28672
R = 512
Z = 8
XY = 16
TILE = 128

decay_keep = 0.05
step_size = 0.5
eps_norm = 1e-06

LIMIT = 52 * 2**20
F32 = jnp.float32
HIGHEST = lax.Precision.HIGHEST


def split_three(values):
    high = values.astype(jnp.bfloat16).astype(F32)
    rest = values - high
    middle = rest.astype(jnp.bfloat16).astype(F32)
    low = (rest - middle).astype(jnp.bfloat16).astype(F32)
    return high, middle, low


def invert_factor_8(entries):
    size = len(entries)
    left = [row[:] for row in entries]
    inverse = [[None] * size for _ in range(size)]
    for j in range(size):
        root = lax.rsqrt(left[j][j])
        square = root * root
        for i in range(j + 1, size):
            share = left[i][j] * square
            for k in range(j + 1, i + 1):
                left[i][k] = left[i][k] - share * left[k][j]
        column = [None] * size
        for i in range(j + 1, size):
            column[i] = left[i][j] * root
        for c in range(j):
            inverse[j][c] = inverse[j][c] * root
        inverse[j][j] = root
        for i in range(j + 1, size):
            for c in range(j + 1):
                term = column[i] * inverse[j][c]
                inverse[i][c] = -term if inverse[i][c] is None else inverse[i][c] - term
    return inverse


def invert_factor_tile(state, result):
    sublane = lax.broadcasted_iota(jnp.int32, (8, TILE), 0)
    lane = lax.broadcasted_iota(jnp.int32, (8, TILE), 1)
    rows = state[0:8, :]
    for step in range(TILE // 8):
        at = 8 * step
        lanes = [jnp.broadcast_to(rows[:, at + j : at + j + 1], (8, TILE)) for j in range(8)]
        entries = [
            [jnp.broadcast_to(lanes[j][i : i + 1, :], (8, TILE)) for j in range(i + 1)] for i in range(8)
        ]
        inverse = invert_factor_8(entries)
        first, second = None, None
        for j in range(8):
            column = jnp.zeros((8, TILE), F32)
            for i in range(j, 8):
                column = jnp.where(sublane == i, inverse[i][j], column)
            one = column * jnp.broadcast_to(rows[j : j + 1, :TILE], (8, TILE))
            two = column * jnp.broadcast_to(rows[j : j + 1, TILE:], (8, TILE))
            first = one if first is None else first + one
            second = two if second is None else second + two
        result[at : at + 8, :] = second
        after = at + 8
        if after == TILE:
            break
        next_first, next_second = state[after : after + 8, :TILE], state[after : after + 8, TILE:]
        for k in range(8):
            one = jnp.broadcast_to(first[k : k + 1, :], (8, TILE))
            two = jnp.broadcast_to(second[k : k + 1, :], (8, TILE))
            factor = jnp.sum(jnp.where(lane == after + sublane, one, 0.0), axis=1, keepdims=True)
            next_first, next_second = next_first - factor * one, next_second - factor * two
        rows = jnp.concatenate([next_first, next_second], 1)
        if after + 8 < TILE:
            high, middle, low = split_three(jnp.concatenate([first, second], 1))
            right = jnp.concatenate([high, middle, high, low, high, middle], 0).astype(jnp.bfloat16)
            high, middle, low = high[:, :TILE], middle[:, :TILE], low[:, :TILE]
            left = jnp.concatenate([high, high, middle, high, low, middle], 0).astype(jnp.bfloat16)
            update = lax.dot_general(left, right, (((0,), (0,)), ((), ())), preferred_element_type=F32)
            state[after + 8 :, :] = state[after + 8 :, :] - update[after + 8 :, :]


def inverse_factor_kernel(gram, earlier, inverse, rest, state, tile):
    rows = lax.broadcasted_iota(jnp.int32, (R, R), 0)
    columns = lax.broadcasted_iota(jnp.int32, (R, R), 1)
    rest[...] = gram[...]
    inverse[...] = jnp.where(rows == columns, 1.0, 0.0)
    identity = jnp.where(
        lax.broadcasted_iota(jnp.int32, (TILE, TILE), 0) == lax.broadcasted_iota(jnp.int32, (TILE, TILE), 1), 1.0, 0.0
    )

    def eliminate(k):
        here, left, right = slice(k * TILE, (k + 1) * TILE), slice(0, (k + 1) * TILE), slice((k + 1) * TILE, R)
        lower = jnp.dot(tile[...], inverse[here, left], precision=HIGHEST, preferred_element_type=F32)
        inverse[here, left] = lower
        if k == R // TILE - 1:
            return
        upper = jnp.dot(tile[...], rest[here, right], precision=HIGHEST, preferred_element_type=F32)
        dims = (((0,), (0,)), ((), ()))
        for i in range(k + 1, R // TILE):
            below = slice(i * TILE, (i + 1) * TILE)
            skip = (i - k - 1) * TILE
            factor = upper[:, skip : skip + TILE]
            rest[below, below.start :] -= lax.dot_general(
                factor, upper[:, skip:], dims, precision=HIGHEST, preferred_element_type=F32
            )
            inverse[below, left] -= lax.dot_general(factor, lower, dims, precision=HIGHEST, preferred_element_type=F32)

    @pl.loop(0, R // TILE)
    def _(k):
        at = pl.multiple_of(k * TILE, TILE)
        state[:, :TILE] = rest[pl.ds(at, TILE), pl.ds(at, TILE)]
        state[:, TILE:] = identity
        invert_factor_tile(state, tile)
        for done in range(R // TILE):

            @pl.when(k == done)
            def _():
                eliminate(done)


def inverse_factor(gram, earlier):
    whole = pl.BlockSpec(memory_space=pltpu.VMEM)
    return pl.pallas_call(
        inverse_factor_kernel,
        out_shape=jax.ShapeDtypeStruct((R, R), F32),
        in_specs=[whole, pl.BlockSpec(memory_space=pl.ANY)],
        out_specs=whole,
        scratch_shapes=[
            pltpu.VMEM((R, R), F32),
            pltpu.VMEM((TILE, 2 * TILE), F32),
            pltpu.VMEM((TILE, TILE), F32),
        ],
        compiler_params=pltpu.CompilerParams(vmem_limit_bytes=12 * 2**20),
        cost_estimate=pl.CostEstimate(flops=3 * 10**10, bytes_accessed=2 * 4 * R * R, transcendentals=R),
        name="inverse_factor",
    )(gram, earlier)


def copy_after(values, earlier):
    def kernel(values_ref, _, out, done):
        copy = pltpu.make_async_copy(values_ref, out, done)
        copy.start()
        copy.wait()

    there = pl.BlockSpec(memory_space=pl.ANY)
    return pl.pallas_call(
        kernel,
        out_shape=jax.ShapeDtypeStruct(values.shape, values.dtype),
        in_specs=[there, there],
        out_specs=there,
        scratch_shapes=[pltpu.SemaphoreType.DMA],
        compiler_params=pltpu.CompilerParams(vmem_limit_bytes=LIMIT),
        cost_estimate=pl.CostEstimate(flops=1, bytes_accessed=2 * 4 * values.size, transcendentals=0),
        name="copy_after",
    )(values, earlier)


def split_two(values):
    high = values.astype(jnp.bfloat16)
    return high, (values - high.astype(F32)).astype(jnp.bfloat16)


def product3(first, second, dims):
    def one(a, b):
        return lax.dot_general(a, b, (dims, ((), ())), preferred_element_type=F32)

    return one(first[0], second[0]) + (one(first[0], second[1]) + one(first[1], second[0]))


WIDTH = 896
NN = ((1,), (0,))
NT = ((1,), (1,))


def call(kernel, steps, operands, specs, outs, out_specs, scratch=(), name=None, flops=3 * 10**9, limit=LIMIT):
    return pl.pallas_call(
        kernel,
        grid=(steps,),
        out_shape=outs,
        in_specs=specs,
        out_specs=out_specs,
        scratch_shapes=list(scratch),
        compiler_params=pltpu.CompilerParams(vmem_limit_bytes=limit, dimension_semantics=("arbitrary",)),
        cost_estimate=pl.CostEstimate(flops=flops, bytes_accessed=4 * 2**20, transcendentals=0),
        name=name,
    )(*operands)


def wide(rows):
    return pl.BlockSpec((rows, WIDTH), lambda j: (0, j))


def whole(*shape):
    return pl.BlockSpec(shape, lambda j: (0,) * len(shape))


def left_product(blocks, chip):
    rows, columns = chip.shape
    ranks = sum(b.shape[0] for b in blocks)

    def kernel(*refs):
        parts, chip_ref, out = refs[:-2], refs[-2], refs[-1]
        right = jnp.concatenate([p[...] for p in parts], 0)
        term = product3(split_two(right), split_two(chip_ref[...]), NT)

        @pl.when(pl.program_id(0) == 0)
        def _():
            out[...] = term

        @pl.when(pl.program_id(0) > 0)
        def _():
            out[...] += term

    return call(
        kernel,
        columns // WIDTH,
        (*blocks, chip),
        [wide(b.shape[0]) for b in blocks] + [wide(rows)],
        jax.ShapeDtypeStruct((ranks, rows), F32),
        whole(ranks, rows),
        name="left_product",
        limit=16 * 2**20,
    )


def right_product(left, chip):
    ranks, rows = left.shape
    columns = chip.shape[1]

    def kernel(left_ref, chip_ref, out, high, low):
        @pl.when(pl.program_id(0) == 0)
        def _():
            high[...], low[...] = split_two(left_ref[...])

        out[...] = product3((high[...], low[...]), split_two(chip_ref[...]), NN)

    half = pltpu.VMEM((ranks, rows), jnp.bfloat16)
    return call(
        kernel,
        columns // WIDTH,
        (left, chip),
        [whole(ranks, rows), wide(rows)],
        jax.ShapeDtypeStruct((ranks, columns), F32),
        wide(ranks),
        (half, half),
        name="right_product",
    )


def right_and_squares(inverse, product):
    columns = product.shape[1]
    steps = columns // WIDTH

    def kernel(inverse_ref, product_ref, out_high, out_low, sums, high, low, total):
        j = pl.program_id(0)

        @pl.when(j == 0)
        def _():
            high[...], low[...] = split_two(inverse_ref[...])
            total[...] = jnp.zeros_like(total)

        right = product3((high[...], low[...]), split_two(product_ref[...]), NN)
        out_high[...], out_low[...] = split_two(right)
        squares = right * right
        total[...] += sum(squares[:, i : i + 128] for i in range(0, WIDTH, 128))

        @pl.when(j == steps - 1)
        def _():
            sums[...] = lax.dot_general(
                jnp.ones((8, 128), F32), total[...], (NT, ((), ())), precision=HIGHEST, preferred_element_type=F32
            )

    half = pltpu.VMEM((R, R), jnp.bfloat16)
    pair = jax.ShapeDtypeStruct((R, columns), jnp.bfloat16)
    return call(
        kernel,
        steps,
        (inverse, product),
        [whole(R, R), wide(R)],
        (pair, pair, jax.ShapeDtypeStruct((8, R), F32)),
        (wide(R), wide(R), whole(8, R)),
        (half, half, pltpu.VMEM((R, 128), F32)),
        name="right_and_squares",
    )


def momentum_update(buffer, ortho, right):
    rows, columns = buffer.shape

    def kernel(buffer_ref, ortho_ref, right_high, right_low, out, high, low):
        @pl.when(pl.program_id(0) == 0)
        def _():
            high[...], low[...] = split_two(ortho_ref[...])

        out[...] = buffer_ref[...] - decay_keep * product3(
            (high[...], low[...]), (right_high[...], right_low[...]), NN
        )

    half = pltpu.VMEM((rows, R), jnp.bfloat16)
    return call(
        kernel,
        columns // WIDTH,
        (buffer, ortho, *right),
        [wide(rows), whole(rows, R), wide(R), wide(R)],
        jax.ShapeDtypeStruct((rows, columns), F32),
        wide(rows),
        (half, half),
        name="momentum_update",
    )


def weights_update(weights, ortho, right, sums, start, share):
    rows, columns = weights.shape
    count = sums.shape[0]

    def kernel(start_ref, weights_ref, ortho_ref, right_high, right_low, sums_ref, out, own, high, low, own_scale):
        at = pl.multiple_of(start_ref[0], share)

        @pl.when(pl.program_id(0) == 0)
        def _():
            scale = jnp.sqrt(jnp.sum(sums_ref[...], axis=0, keepdims=True) / N + eps_norm)
            high[...], low[...] = split_two(ortho_ref[...] / scale)
            lanes = lax.broadcasted_iota(jnp.int32, (share, R), 1)
            chosen = lanes == at + lax.broadcasted_iota(jnp.int32, (share, R), 0)
            picked = jnp.sum(jnp.where(chosen, jnp.broadcast_to(scale, (share, R)), 0.0), axis=1, keepdims=True)
            own_scale[...] = jnp.broadcast_to(picked, own_scale.shape)

        out[...] = weights_ref[...] - step_size * product3(
            (high[...], low[...]), (right_high[...], right_low[...]), NN
        )
        here = pl.ds(at, share)
        own[...] = (right_high[here, :].astype(F32) + right_low[here, :].astype(F32)) / own_scale[...]

    half = pltpu.VMEM((rows, R), jnp.bfloat16)
    return call(
        kernel,
        columns // WIDTH,
        (start, weights, ortho, *right, sums),
        [pl.BlockSpec(memory_space=pltpu.SMEM), wide(rows), whole(rows, R), wide(R), wide(R), whole(count, R)],
        (jax.ShapeDtypeStruct((rows, columns), F32), jax.ShapeDtypeStruct((share, columns), F32)),
        (wide(rows), wide(share)),
        (half, half, pltpu.VMEM((share, WIDTH), F32)),
        name="weights_update",
    )


SIZES = {"z": Z, "core": 2, "x": 4, "y": 4}


def shift(values, axis, by):
    size = SIZES[axis]
    return lax.ppermute(values, axis, [(i, (i + by) % size) for i in range(size)])


def spread(values, axes, count):
    whole = jnp.broadcast_to(values[None], (count,) + values.shape)
    return lax.all_to_all(whole, axes, 0, 0, tiled=True)


def gather_z(own):
    half = own.shape[0] // 2
    below1, above1 = shift(own, "z", 1), shift(own, "z", -1)
    below2, above2 = shift(own, "z", 2), shift(own, "z", -2)
    below3, above3 = shift(below2, "z", 1), shift(above2, "z", -1)
    across = (shift(below3[:half], "z", 1), shift(above3[half:], "z", -1))
    return [own, above1, above2, above3, across, below3, below2, below1]


def dot(first, second, dims, precision):
    return lax.dot_general(
        first, second, ((dims[0], dims[1]), ((), ())), precision=precision, preferred_element_type=F32
    )


def local(weights, momentum, gradient, right_factor):
    core = lax.axis_index("core")
    plane = lax.axis_index("x") * 4 + lax.axis_index("y")
    z = lax.axis_index("z")
    share = right_factor.shape[0]

    buffer = momentum + gradient.astype(F32)
    right = gather_z(right_factor)
    beside = shift(buffer, "core", 1)
    chip = jnp.where(
        core == 0, jnp.concatenate([buffer, beside], 0), jnp.concatenate([beside, buffer], 0)
    )

    blocks = [*right[:4], *right[4], *right[5:]]
    part = left_product(blocks, chip)
    rows = part.shape[1]
    pieces = lax.all_to_all(part.reshape(XY, -1, rows), ("x", "y"), 0, 0, tiled=True)
    left = spread(jnp.sum(pieces, 0), ("x", "y"), XY).reshape(Z, share, rows)
    own = lax.dynamic_slice_in_dim(jnp.concatenate([left, left], 0), (Z - z) % Z, Z, 0)

    product = right_product(own.reshape(Z * share, rows), chip)
    product = lax.psum_scatter(product, "z", scatter_dimension=0, tiled=True)

    other = shift(own, "core", 1)
    left_all = jnp.stack([jnp.where(core == 0, own, other), jnp.where(core == 0, other, own)], 1)
    left_all = left_all.reshape(R, rows)
    height = R // (2 * XY)
    mine = lax.dynamic_slice_in_dim(left_all, (core * XY + plane) * height, height, 0)
    gram = jnp.sum(spread(dot(mine, left_all, ((1,), (1,)), HIGHEST), "z", Z), 0)
    gram = spread(gram, ("x", "y"), XY).reshape(R // 2, R)
    gram_other = shift(gram, "core", 1)
    gram = jnp.where(
        core == 0, jnp.concatenate([gram, gram_other], 0), jnp.concatenate([gram_other, gram], 0)
    )
    product = copy_after(product, gram)
    inverse = inverse_factor(gram, product)
    product = lax.all_gather(product, ("z", "core"), axis=0, tiled=True)

    height = rows // 2
    left_own = jnp.where(core == 0, left_all[:, :height], left_all[:, height:])
    ortho = dot(left_own, inverse, ((0,), (1,)), HIGHEST)
    *right_t, sums = right_and_squares(inverse, product)
    sums = spread(sums[:1], ("x", "y"), XY).reshape(XY, R)
    start = jnp.full((1,), (2 * z + core) * share, jnp.int32)
    new_momentum = momentum_update(buffer, ortho, right_t)
    new_weights, new_right = weights_update(weights, ortho, right_t, sums, start, share)
    return (new_weights, new_momentum, new_right)


def solution(mesh):
    fine = Mesh(mesh.devices.reshape(Z, 2, 4, 4), ("z", "core", "x", "y"))
    spec = P(("z", "core"), ("x", "y"))
    return jax.shard_map(
        local, mesh=fine, in_specs=(spec, spec, spec, spec), out_specs=(spec, spec, spec), check_vma=False
    )
```

```python
import jax
import jax.numpy as jnp
from jax import lax
from jax.experimental import pallas as pl
from jax.experimental.pallas import tpu as pltpu
from jax.sharding import Mesh, PartitionSpec as P

N = 28672
R = 512
Z = 8
XY = 16
TILE = 128

decay_keep = 0.05
step_size = 0.5
eps_norm = 1e-06

LIMIT = 52 * 2**20
F32 = jnp.float32
HIGHEST = lax.Precision.HIGHEST


def split_three(values):
    high = values.astype(jnp.bfloat16).astype(F32)
    rest = values - high
    middle = rest.astype(jnp.bfloat16).astype(F32)
    low = (rest - middle).astype(jnp.bfloat16).astype(F32)
    return high, middle, low


def invert_factor_8(entries):
    size = len(entries)
    left = [row[:] for row in entries]
    inverse = [[None] * size for _ in range(size)]
    for j in range(size):
        root = lax.rsqrt(left[j][j])
        square = root * root
        for i in range(j + 1, size):
            share = left[i][j] * square
            for k in range(j + 1, i + 1):
                left[i][k] = left[i][k] - share * left[k][j]
        column = [None] * size
        for i in range(j + 1, size):
            column[i] = left[i][j] * root
        for c in range(j):
            inverse[j][c] = inverse[j][c] * root
        inverse[j][j] = root
        for i in range(j + 1, size):
            for c in range(j + 1):
                term = column[i] * inverse[j][c]
                inverse[i][c] = -term if inverse[i][c] is None else inverse[i][c] - term
    return inverse


def invert_factor_tile(state, result):
    sublane = lax.broadcasted_iota(jnp.int32, (8, TILE), 0)
    lane = lax.broadcasted_iota(jnp.int32, (8, TILE), 1)
    rows = state[0:8, :]
    for step in range(TILE // 8):
        at = 8 * step
        lanes = [jnp.broadcast_to(rows[:, at + j : at + j + 1], (8, TILE)) for j in range(8)]
        entries = [
            [jnp.broadcast_to(lanes[j][i : i + 1, :], (8, TILE)) for j in range(i + 1)] for i in range(8)
        ]
        inverse = invert_factor_8(entries)
        first, second = None, None
        for j in range(8):
            column = jnp.zeros((8, TILE), F32)
            for i in range(j, 8):
                column = jnp.where(sublane == i, inverse[i][j], column)
            one = column * jnp.broadcast_to(rows[j : j + 1, :TILE], (8, TILE))
            two = column * jnp.broadcast_to(rows[j : j + 1, TILE:], (8, TILE))
            first = one if first is None else first + one
            second = two if second is None else second + two
        result[at : at + 8, :] = second
        after = at + 8
        if after == TILE:
            break
        next_first, next_second = state[after : after + 8, :TILE], state[after : after + 8, TILE:]
        for k in range(8):
            one = jnp.broadcast_to(first[k : k + 1, :], (8, TILE))
            two = jnp.broadcast_to(second[k : k + 1, :], (8, TILE))
            factor = jnp.sum(jnp.where(lane == after + sublane, one, 0.0), axis=1, keepdims=True)
            next_first, next_second = next_first - factor * one, next_second - factor * two
        rows = jnp.concatenate([next_first, next_second], 1)
        if after + 8 < TILE:
            high, middle, low = split_three(jnp.concatenate([first, second], 1))
            right = jnp.concatenate([high, middle, high, low, high, middle], 0).astype(jnp.bfloat16)
            high, middle, low = high[:, :TILE], middle[:, :TILE], low[:, :TILE]
            left = jnp.concatenate([high, high, middle, high, low, middle], 0).astype(jnp.bfloat16)
            update = lax.dot_general(left, right, (((0,), (0,)), ((), ())), preferred_element_type=F32)
            state[after + 8 :, :] = state[after + 8 :, :] - update[after + 8 :, :]


def inverse_factor_kernel(gram, earlier, result, inverse, rest, state, tile):
    rows = lax.broadcasted_iota(jnp.int32, (R, R), 0)
    columns = lax.broadcasted_iota(jnp.int32, (R, R), 1)
    rest[...] = gram[...]
    inverse[...] = jnp.where(rows == columns, 1.0, 0.0)
    identity = jnp.where(
        lax.broadcasted_iota(jnp.int32, (TILE, TILE), 0) == lax.broadcasted_iota(jnp.int32, (TILE, TILE), 1), 1.0, 0.0
    )

    def eliminate(k):
        here, left, right = slice(k * TILE, (k + 1) * TILE), slice(0, (k + 1) * TILE), slice((k + 1) * TILE, R)
        lower = jnp.dot(tile[...], inverse[here, left], precision=HIGHEST, preferred_element_type=F32)
        inverse[here, left] = lower
        if k == R // TILE - 1:
            return
        upper = jnp.dot(tile[...], rest[here, right], precision=HIGHEST, preferred_element_type=F32)
        dims = (((0,), (0,)), ((), ()))
        for i in range(k + 1, R // TILE):
            below = slice(i * TILE, (i + 1) * TILE)
            skip = (i - k - 1) * TILE
            factor = upper[:, skip : skip + TILE]
            rest[below, below.start :] -= lax.dot_general(
                factor, upper[:, skip:], dims, precision=HIGHEST, preferred_element_type=F32
            )
            inverse[below, left] -= lax.dot_general(factor, lower, dims, precision=HIGHEST, preferred_element_type=F32)

    @pl.loop(0, R // TILE)
    def _(k):
        at = pl.multiple_of(k * TILE, TILE)
        state[:, :TILE] = rest[pl.ds(at, TILE), pl.ds(at, TILE)]
        state[:, TILE:] = identity
        invert_factor_tile(state, tile)
        for done in range(R // TILE):

            @pl.when(k == done)
            def _():
                eliminate(done)

    share = R // (2 * Z)
    core, chip, place = columns // (R // 2), columns // share % Z, columns % share
    chosen = jnp.where(rows == (2 * chip + core) * share + place, 1.0, 0.0).astype(jnp.bfloat16)
    parts = [part.astype(jnp.bfloat16) for part in split_three(inverse[...])]
    high, middle, low = (jnp.dot(part, chosen, preferred_element_type=F32) for part in parts)
    result[...] = high + (middle + low)


def inverse_factor(gram, earlier):
    whole = pl.BlockSpec(memory_space=pltpu.VMEM)
    return pl.pallas_call(
        inverse_factor_kernel,
        out_shape=jax.ShapeDtypeStruct((R, R), F32),
        in_specs=[whole, pl.BlockSpec(memory_space=pl.ANY)],
        out_specs=whole,
        scratch_shapes=[
            pltpu.VMEM((R, R), F32),
            pltpu.VMEM((R, R), F32),
            pltpu.VMEM((TILE, 2 * TILE), F32),
            pltpu.VMEM((TILE, TILE), F32),
        ],
        compiler_params=pltpu.CompilerParams(vmem_limit_bytes=12 * 2**20),
        cost_estimate=pl.CostEstimate(flops=3 * 10**10, bytes_accessed=2 * 4 * R * R, transcendentals=R),
        name="inverse_factor",
    )(gram, earlier)


def copy_after(values, earlier):
    def kernel(values_ref, _, out, done):
        copy = pltpu.make_async_copy(values_ref, out, done)
        copy.start()
        copy.wait()

    there = pl.BlockSpec(memory_space=pltpu.HBM)
    return pl.pallas_call(
        kernel,
        out_shape=jax.ShapeDtypeStruct(values.shape, values.dtype),
        in_specs=[there, pl.BlockSpec(memory_space=pl.ANY)],
        out_specs=there,
        scratch_shapes=[pltpu.SemaphoreType.DMA],
        compiler_params=pltpu.CompilerParams(vmem_limit_bytes=LIMIT),
        cost_estimate=pl.CostEstimate(flops=1, bytes_accessed=2 * 4 * values.size, transcendentals=0),
        name="copy_after",
    )(values, earlier)


def split_two(values):
    high = values.astype(jnp.bfloat16)
    return high, (values - high.astype(F32)).astype(jnp.bfloat16)


def product3(first, second, dims):
    def one(a, b):
        return lax.dot_general(a, b, (dims, ((), ())), preferred_element_type=F32)

    return one(first[0], second[0]) + (one(first[0], second[1]) + one(first[1], second[0]))


WIDTH = 896
NN = ((1,), (0,))
NT = ((1,), (1,))


def call(kernel, steps, operands, specs, outs, out_specs, scratch=(), name=None, flops=3 * 10**9, limit=LIMIT):
    return pl.pallas_call(
        kernel,
        grid=(steps,),
        out_shape=outs,
        in_specs=specs,
        out_specs=out_specs,
        scratch_shapes=list(scratch),
        compiler_params=pltpu.CompilerParams(vmem_limit_bytes=limit, dimension_semantics=("arbitrary",)),
        cost_estimate=pl.CostEstimate(flops=flops, bytes_accessed=4 * 2**20, transcendentals=0),
        name=name,
    )(*operands)


def wide(rows):
    return pl.BlockSpec((rows, WIDTH), lambda j: (0, j))


def whole(*shape):
    return pl.BlockSpec(shape, lambda j: (0,) * len(shape))


def left_product(blocks, chip):
    rows, columns = chip.shape
    ranks = sum(b.shape[0] for b in blocks)

    def kernel(*refs):
        parts, chip_ref, out = refs[:-2], refs[-2], refs[-1]
        right = jnp.concatenate([p[...] for p in parts], 0)
        term = product3(split_two(right), split_two(chip_ref[...]), NT)

        @pl.when(pl.program_id(0) == 0)
        def _():
            out[...] = term

        @pl.when(pl.program_id(0) > 0)
        def _():
            out[...] += term

    return call(
        kernel,
        columns // WIDTH,
        (*blocks, chip),
        [wide(b.shape[0]) for b in blocks] + [wide(rows)],
        jax.ShapeDtypeStruct((ranks, rows), F32),
        whole(ranks, rows),
        name="left_product",
        limit=16 * 2**20,
    )


def right_product(left, chip):
    ranks, rows = left.shape
    columns = chip.shape[1]

    def kernel(left_ref, chip_ref, out, high, low):
        @pl.when(pl.program_id(0) == 0)
        def _():
            high[...], low[...] = split_two(left_ref[...])

        out[...] = product3((high[...], low[...]), split_two(chip_ref[...]), NN).T

    half = pltpu.VMEM((ranks, rows), jnp.bfloat16)
    return call(
        kernel,
        columns // WIDTH,
        (left, chip),
        [whole(ranks, rows), wide(rows)],
        jax.ShapeDtypeStruct((columns, ranks), F32),
        pl.BlockSpec((WIDTH, ranks), lambda j: (j, 0)),
        (half, half),
        name="right_product",
    )


def column_squares(inverse, own, other, core):
    def kernel(core_ref, inverse_ref, own_ref, other_ref, sums):
        mine = core_ref[0] == 0
        first = jnp.where(mine, own_ref[...], other_ref[...])
        second = jnp.where(mine, other_ref[...], own_ref[...])
        product = jnp.concatenate([first, second], 1)
        right = product3(split_two(product), split_two(inverse_ref[...]), NT)
        sums[...] = jnp.broadcast_to(jnp.sum(right * right, axis=0, keepdims=True), sums.shape)

    vmem = pl.BlockSpec(memory_space=pltpu.VMEM)
    return pl.pallas_call(
        kernel,
        out_shape=jax.ShapeDtypeStruct((Z, 1, R), F32),
        in_specs=[pl.BlockSpec(memory_space=pltpu.SMEM), vmem, vmem, vmem],
        out_specs=vmem,
        compiler_params=pltpu.CompilerParams(vmem_limit_bytes=16 * 2**20),
        cost_estimate=pl.CostEstimate(flops=10**9, bytes_accessed=2**20, transcendentals=0),
        name="column_squares",
    )(core, inverse, own, other)


def total_after(sums, earlier):
    def kernel(sums_ref, _, out):
        out[...] = jnp.broadcast_to(jnp.sum(sums_ref[...], axis=0, keepdims=True), out.shape)

    vmem = pl.BlockSpec(memory_space=pltpu.VMEM)
    return pl.pallas_call(
        kernel,
        out_shape=jax.ShapeDtypeStruct((XY, 1, R), F32),
        in_specs=[vmem, pl.BlockSpec(memory_space=pl.ANY)],
        out_specs=vmem,
        compiler_params=pltpu.CompilerParams(vmem_limit_bytes=LIMIT),
        cost_estimate=pl.CostEstimate(flops=1, bytes_accessed=2**16, transcendentals=0),
        name="total_after",
    )(sums, earlier)


def momentum_update(buffer, ortho, inverse, product):
    rows, columns = buffer.shape
    count = WIDTH // product.shape[2]

    def kernel(buffer_ref, ortho_ref, inverse_ref, product_ref, out, out_high, out_low, *halves):
        left, inner = halves[:2], halves[2:]

        @pl.when(pl.program_id(0) == 0)
        def _():
            left[0][...], left[1][...] = split_two(ortho_ref[...])
            inner[0][...], inner[1][...] = split_two(inverse_ref[...])

        ranks = product.shape[3]
        block = jnp.concatenate([product_ref[:, c].reshape(WIDTH, ranks) for c in range(2)], 1)
        right = product3(split_two(block), (inner[0][...], inner[1][...]), NT)
        high, low = split_two(right)
        out_high[...], out_low[...] = high, low
        out[...] = buffer_ref[...] - decay_keep * product3((left[0][...], left[1][...]), (high, low), NT)

    half, square = pltpu.VMEM((rows, R), jnp.bfloat16), pltpu.VMEM((R, R), jnp.bfloat16)
    pair = jax.ShapeDtypeStruct((columns, R), jnp.bfloat16)
    tall = pl.BlockSpec((WIDTH, R), lambda j: (j, 0))
    return call(
        kernel,
        columns // WIDTH,
        (buffer, ortho, inverse, product),
        [
            wide(rows),
            whole(rows, R),
            whole(R, R),
            pl.BlockSpec((count, *product.shape[1:]), lambda j: (j, 0, 0, 0)),
        ],
        (jax.ShapeDtypeStruct((rows, columns), F32), pair, pair),
        (wide(rows), tall, tall),
        (half, half, square, square),
        name="momentum_update",
    )


def weights_update(weights, ortho, right, sums, start, share):
    rows, columns = weights.shape
    count = sums.shape[0]

    def kernel(start_ref, weights_ref, ortho_ref, right_high, right_low, sums_ref, out, own, high, low, chosen, own_scale):
        @pl.when(pl.program_id(0) == 0)
        def _():
            scale = jnp.sqrt(jnp.sum(sums_ref[...], axis=0) / N + eps_norm)
            high[...], low[...] = split_two(ortho_ref[...] / scale)
            lanes = lax.broadcasted_iota(jnp.int32, (share, R), 1)
            mine = lanes == start_ref[0] + lax.broadcasted_iota(jnp.int32, (share, R), 0)
            chosen[...] = jnp.where(mine, 1.0, 0.0).astype(jnp.bfloat16)
            picked = jnp.sum(jnp.where(mine, jnp.broadcast_to(scale, (share, R)), 0.0), axis=1, keepdims=True)
            own_scale[...] = jnp.broadcast_to(picked, own_scale.shape)

        right = right_high[...], right_low[...]
        out[...] = weights_ref[...] - step_size * product3((high[...], low[...]), right, NT)
        rows_high, rows_low = (
            lax.dot_general(chosen[...], one, (NT, ((), ())), preferred_element_type=F32) for one in right
        )
        own[...] = (rows_high + rows_low) / own_scale[...]

    half = pltpu.VMEM((rows, R), jnp.bfloat16)
    tall = pl.BlockSpec((WIDTH, R), lambda j: (j, 0))
    return call(
        kernel,
        columns // WIDTH,
        (start, weights, ortho, *right, sums),
        [pl.BlockSpec(memory_space=pltpu.SMEM), wide(rows), whole(rows, R), tall, tall, whole(count, 1, R)],
        (jax.ShapeDtypeStruct((rows, columns), F32), jax.ShapeDtypeStruct((share, columns), F32)),
        (wide(rows), wide(share)),
        (half, half, pltpu.VMEM((share, R), jnp.bfloat16), pltpu.VMEM((share, WIDTH), F32)),
        name="weights_update",
    )


SIZES = {"z": Z, "core": 2, "x": 4, "y": 4}


def shift(values, axis, by):
    size = SIZES[axis]
    return lax.ppermute(values, axis, [(i, (i + by) % size) for i in range(size)])


def spread(values, axes, count):
    whole = jnp.broadcast_to(values[None], (count,) + values.shape)
    return lax.all_to_all(whole, axes, 0, 0, tiled=True)


def gather_z(own):
    half = own.shape[0] // 2
    below1, above1 = shift(own, "z", 1), shift(own, "z", -1)
    below2, above2 = shift(own, "z", 2), shift(own, "z", -2)
    below3, above3 = shift(below2, "z", 1), shift(above2, "z", -1)
    across = (shift(below2[:half], "z", 2), shift(above2[half:], "z", -2))
    return [own, above1, above2, above3, across, below3, below2, below1]


def dot(first, second, dims, precision):
    return lax.dot_general(
        first, second, ((dims[0], dims[1]), ((), ())), precision=precision, preferred_element_type=F32
    )


def local(weights, momentum, gradient, right_factor):
    core = lax.axis_index("core")
    plane = lax.axis_index("x") * 4 + lax.axis_index("y")
    z = lax.axis_index("z")
    share = right_factor.shape[0]

    buffer = momentum + gradient.astype(F32)
    right = gather_z(right_factor)
    beside = shift(buffer, "core", 1)
    chip = jnp.where(
        core == 0, jnp.concatenate([buffer, beside], 0), jnp.concatenate([beside, buffer], 0)
    )

    blocks = [*right[:4], *right[4], *right[5:]]
    part = left_product(blocks, chip)
    rows = part.shape[1]
    pieces = lax.all_to_all(part.reshape(XY, -1, rows), ("x", "y"), 0, 0, tiled=True)
    left = spread(jnp.sum(pieces, 0), ("x", "y"), XY).reshape(Z, share, rows)
    own = lax.dynamic_slice_in_dim(jnp.concatenate([left, left], 0), (Z - z) % Z, Z, 0)

    product = right_product(own.reshape(Z * share, rows), chip)
    product = lax.psum_scatter(product, "z", scatter_dimension=0, tiled=True)

    other = shift(own, "core", 1)
    by_core = [jnp.where(core == 0, own, other), jnp.where(core == 0, other, own)]
    left_all = jnp.stack(by_core, 1).reshape(R, rows)
    height = R // (2 * XY)
    mine = lax.dynamic_slice_in_dim(left_all, (core * XY + plane) * height, height, 0)
    gram = jnp.sum(spread(dot(mine, left_all, ((1,), (1,)), HIGHEST), "z", Z), 0)
    gram = spread(gram, ("x", "y"), XY).reshape(R // 2, R)
    gram_other = shift(gram, "core", 1)
    gram = jnp.where(
        core == 0, jnp.concatenate([gram, gram_other], 0), jnp.concatenate([gram_other, gram], 0)
    )
    product = copy_after(product, gram)
    inverse = inverse_factor(gram, product)

    beside = shift(product, "core", 1)
    sums = column_squares(inverse, product, beside, jnp.full((1,), core, jnp.int32))
    sums = lax.all_to_all(sums, "z", 0, 0, tiled=True)
    product = lax.all_gather(product, ("z", "core"), axis=0, tiled=True)
    product = product.reshape(Z, 2, -1, product.shape[1])

    height = rows // 2
    left_own = jnp.concatenate(by_core, 0).reshape(R, rows)
    left_own = jnp.where(core == 0, left_own[:, :height], left_own[:, height:])
    ortho = dot(left_own, inverse, ((0,), (1,)), HIGHEST)
    sums = lax.all_to_all(total_after(sums, product), ("x", "y"), 0, 0, tiled=True)
    new_momentum, *right_t = momentum_update(buffer, ortho, inverse, product)
    start = jnp.full((1,), (2 * z + core) * share, jnp.int32)
    new_weights, new_right = weights_update(weights, ortho, right_t, sums, start, share)
    return (new_weights, new_momentum, new_right)


def solution(mesh):
    fine = Mesh(mesh.devices.reshape(Z, 2, 4, 4), ("z", "core", "x", "y"))
    spec = P(("z", "core"), ("x", "y"))
    return jax.shard_map(
        local, mesh=fine, in_specs=(spec, spec, spec, spec), out_specs=(spec, spec, spec), check_vma=False
    )
```

```python
import jax
import jax.numpy as jnp
from jax import lax
from jax.experimental import pallas as pl
from jax.experimental.pallas import tpu as pltpu
from jax.sharding import Mesh, PartitionSpec as P

N = 28672
R = 512
Z = 8
XY = 16
TILE = 128

decay_keep = 0.05
step_size = 0.5
eps_norm = 1e-06

LIMIT = 52 * 2**20
F32 = jnp.float32
HIGHEST = lax.Precision.HIGHEST


def split_three(values):
    high = values.astype(jnp.bfloat16).astype(F32)
    rest = values - high
    middle = rest.astype(jnp.bfloat16).astype(F32)
    low = (rest - middle).astype(jnp.bfloat16).astype(F32)
    return high, middle, low


def invert_factor_8(entries):
    size = len(entries)
    left = [row[:] for row in entries]
    inverse = [[None] * size for _ in range(size)]
    for j in range(size):
        root = lax.rsqrt(left[j][j])
        square = root * root
        for i in range(j + 1, size):
            share = left[i][j] * square
            for k in range(j + 1, i + 1):
                left[i][k] = left[i][k] - share * left[k][j]
        column = [None] * size
        for i in range(j + 1, size):
            column[i] = left[i][j] * root
        for c in range(j):
            inverse[j][c] = inverse[j][c] * root
        inverse[j][j] = root
        for i in range(j + 1, size):
            for c in range(j + 1):
                term = column[i] * inverse[j][c]
                inverse[i][c] = -term if inverse[i][c] is None else inverse[i][c] - term
    return inverse


def invert_factor_tile(state, result):
    sublane = lax.broadcasted_iota(jnp.int32, (8, TILE), 0)
    lane = lax.broadcasted_iota(jnp.int32, (8, TILE), 1)
    rows = state[0:8, :]
    for step in range(TILE // 8):
        at = 8 * step
        lanes = [jnp.broadcast_to(rows[:, at + j : at + j + 1], (8, TILE)) for j in range(8)]
        entries = [
            [jnp.broadcast_to(lanes[j][i : i + 1, :], (8, TILE)) for j in range(i + 1)] for i in range(8)
        ]
        inverse = invert_factor_8(entries)
        first, second = None, None
        for j in range(8):
            column = jnp.zeros((8, TILE), F32)
            for i in range(j, 8):
                column = jnp.where(sublane == i, inverse[i][j], column)
            one = column * jnp.broadcast_to(rows[j : j + 1, :TILE], (8, TILE))
            two = column * jnp.broadcast_to(rows[j : j + 1, TILE:], (8, TILE))
            first = one if first is None else first + one
            second = two if second is None else second + two
        result[at : at + 8, :] = second
        after = at + 8
        if after == TILE:
            break
        next_first, next_second = state[after : after + 8, :TILE], state[after : after + 8, TILE:]
        for k in range(8):
            one = jnp.broadcast_to(first[k : k + 1, :], (8, TILE))
            two = jnp.broadcast_to(second[k : k + 1, :], (8, TILE))
            factor = jnp.sum(jnp.where(lane == after + sublane, one, 0.0), axis=1, keepdims=True)
            next_first, next_second = next_first - factor * one, next_second - factor * two
        rows = jnp.concatenate([next_first, next_second], 1)
        if after + 8 < TILE:
            high, middle, low = split_three(jnp.concatenate([first, second], 1))
            right = jnp.concatenate([high, middle, high, low, high, middle], 0).astype(jnp.bfloat16)
            high, middle, low = high[:, :TILE], middle[:, :TILE], low[:, :TILE]
            left = jnp.concatenate([high, high, middle, high, low, middle], 0).astype(jnp.bfloat16)
            update = lax.dot_general(left, right, (((0,), (0,)), ((), ())), preferred_element_type=F32)
            state[after + 8 :, :] = state[after + 8 :, :] - update[after + 8 :, :]


def inverse_factor_kernel(gram, earlier, result, inverse, rest, state, tile):
    rows = lax.broadcasted_iota(jnp.int32, (R, R), 0)
    columns = lax.broadcasted_iota(jnp.int32, (R, R), 1)
    rest[...] = gram[...]
    inverse[...] = jnp.where(rows == columns, 1.0, 0.0)
    identity = jnp.where(
        lax.broadcasted_iota(jnp.int32, (TILE, TILE), 0) == lax.broadcasted_iota(jnp.int32, (TILE, TILE), 1), 1.0, 0.0
    )

    def eliminate(k):
        here, left, right = slice(k * TILE, (k + 1) * TILE), slice(0, (k + 1) * TILE), slice((k + 1) * TILE, R)
        lower = jnp.dot(tile[...], inverse[here, left], precision=HIGHEST, preferred_element_type=F32)
        inverse[here, left] = lower
        if k == R // TILE - 1:
            return
        upper = jnp.dot(tile[...], rest[here, right], precision=HIGHEST, preferred_element_type=F32)
        dims = (((0,), (0,)), ((), ()))
        for i in range(k + 1, R // TILE):
            below = slice(i * TILE, (i + 1) * TILE)
            skip = (i - k - 1) * TILE
            factor = upper[:, skip : skip + TILE]
            rest[below, below.start :] -= lax.dot_general(
                factor, upper[:, skip:], dims, precision=HIGHEST, preferred_element_type=F32
            )
            inverse[below, left] -= lax.dot_general(factor, lower, dims, precision=HIGHEST, preferred_element_type=F32)

    @pl.loop(0, R // TILE)
    def _(k):
        at = pl.multiple_of(k * TILE, TILE)
        state[:, :TILE] = rest[pl.ds(at, TILE), pl.ds(at, TILE)]
        state[:, TILE:] = identity
        invert_factor_tile(state, tile)
        for done in range(R // TILE):

            @pl.when(k == done)
            def _():
                eliminate(done)

    share = R // (2 * Z)
    core, chip, place = columns // (R // 2), columns // share % Z, columns % share
    chosen = jnp.where(rows == (2 * chip + core) * share + place, 1.0, 0.0).astype(jnp.bfloat16)
    parts = [part.astype(jnp.bfloat16) for part in split_three(inverse[...])]
    high, middle, low = (jnp.dot(part, chosen, preferred_element_type=F32) for part in parts)
    result[...] = high + (middle + low)


def inverse_factor(gram, earlier):
    whole = pl.BlockSpec(memory_space=pltpu.VMEM)
    return pl.pallas_call(
        inverse_factor_kernel,
        out_shape=jax.ShapeDtypeStruct((R, R), F32),
        in_specs=[whole, pl.BlockSpec(memory_space=pl.ANY)],
        out_specs=whole,
        scratch_shapes=[
            pltpu.VMEM((R, R), F32),
            pltpu.VMEM((R, R), F32),
            pltpu.VMEM((TILE, 2 * TILE), F32),
            pltpu.VMEM((TILE, TILE), F32),
        ],
        compiler_params=pltpu.CompilerParams(vmem_limit_bytes=12 * 2**20),
        cost_estimate=pl.CostEstimate(flops=3 * 10**10, bytes_accessed=2 * 4 * R * R, transcendentals=R),
        name="inverse_factor",
    )(gram, earlier)


def after(values, earlier):
    tile = (slice(0, 8), slice(0, 128))
    first = jnp.where(earlier[tile] == earlier[tile], values[tile], earlier[tile])
    return lax.dynamic_update_slice(values, first, (0, 0))


def split_two(values):
    high = values.astype(jnp.bfloat16)
    return high, (values - high.astype(F32)).astype(jnp.bfloat16)


def product3(first, second, dims):
    def one(a, b):
        return lax.dot_general(a, b, (dims, ((), ())), preferred_element_type=F32)

    return one(first[0], second[0]) + (one(first[0], second[1]) + one(first[1], second[0]))


WIDTH = 896
NN = ((1,), (0,))
NT = ((1,), (1,))


def call(kernel, steps, operands, specs, outs, out_specs, scratch=(), name=None, flops=3 * 10**9, limit=LIMIT):
    return pl.pallas_call(
        kernel,
        grid=(steps,),
        out_shape=outs,
        in_specs=specs,
        out_specs=out_specs,
        scratch_shapes=list(scratch),
        compiler_params=pltpu.CompilerParams(vmem_limit_bytes=limit, dimension_semantics=("arbitrary",)),
        cost_estimate=pl.CostEstimate(flops=flops, bytes_accessed=4 * 2**20, transcendentals=0),
        name=name,
    )(*operands)


def wide(rows):
    return pl.BlockSpec((rows, WIDTH), lambda j: (0, j))


def whole(*shape):
    return pl.BlockSpec(shape, lambda j: (0,) * len(shape))


def left_product(blocks, chip):
    rows, columns = chip.shape
    ranks = sum(b.shape[0] for b in blocks)

    def kernel(*refs):
        parts, chip_ref, out = refs[:-2], refs[-2], refs[-1]
        right = jnp.concatenate([p[...] for p in parts], 0)
        term = product3(split_two(right), split_two(chip_ref[...]), NT)

        @pl.when(pl.program_id(0) == 0)
        def _():
            out[...] = term

        @pl.when(pl.program_id(0) > 0)
        def _():
            out[...] += term

    return call(
        kernel,
        columns // WIDTH,
        (*blocks, chip),
        [wide(b.shape[0]) for b in blocks] + [wide(rows)],
        jax.ShapeDtypeStruct((ranks, rows), F32),
        whole(ranks, rows),
        name="left_product",
        limit=16 * 2**20,
    )


def right_product(left, chip):
    ranks, rows = left.shape
    columns = chip.shape[1]

    def kernel(left_ref, chip_ref, out, high, low):
        @pl.when(pl.program_id(0) == 0)
        def _():
            high[...], low[...] = split_two(left_ref[...])

        out[...] = product3((high[...], low[...]), split_two(chip_ref[...]), NN).T

    half = pltpu.VMEM((ranks, rows), jnp.bfloat16)
    return call(
        kernel,
        columns // WIDTH,
        (left, chip),
        [whole(ranks, rows), wide(rows)],
        jax.ShapeDtypeStruct((columns, ranks), F32),
        pl.BlockSpec((WIDTH, ranks), lambda j: (j, 0)),
        (half, half),
        name="right_product",
    )


def column_squares(inverse, own, other, core):
    def kernel(core_ref, inverse_ref, own_ref, other_ref, sums):
        mine = core_ref[0] == 0
        first = jnp.where(mine, own_ref[...], other_ref[...])
        second = jnp.where(mine, other_ref[...], own_ref[...])
        product = jnp.concatenate([first, second], 1)
        right = product3(split_two(product), split_two(inverse_ref[...]), NT)
        sums[...] = jnp.broadcast_to(jnp.sum(right * right, axis=0, keepdims=True), sums.shape)

    vmem = pl.BlockSpec(memory_space=pltpu.VMEM)
    return pl.pallas_call(
        kernel,
        out_shape=jax.ShapeDtypeStruct((Z, 1, R), F32),
        in_specs=[pl.BlockSpec(memory_space=pltpu.SMEM), vmem, vmem, vmem],
        out_specs=vmem,
        compiler_params=pltpu.CompilerParams(vmem_limit_bytes=16 * 2**20),
        cost_estimate=pl.CostEstimate(flops=10**9, bytes_accessed=2**20, transcendentals=0),
        name="column_squares",
    )(core, inverse, own, other)


def total_after(sums, earlier):
    def kernel(sums_ref, _, out):
        out[...] = jnp.broadcast_to(jnp.sum(sums_ref[...], axis=0, keepdims=True), out.shape)

    vmem = pl.BlockSpec(memory_space=pltpu.VMEM)
    return pl.pallas_call(
        kernel,
        out_shape=jax.ShapeDtypeStruct((XY, 1, R), F32),
        in_specs=[vmem, pl.BlockSpec(memory_space=pl.ANY)],
        out_specs=vmem,
        compiler_params=pltpu.CompilerParams(vmem_limit_bytes=LIMIT),
        cost_estimate=pl.CostEstimate(flops=1, bytes_accessed=2**16, transcendentals=0),
        name="total_after",
    )(sums, earlier)


def columns_first(product_ref):
    count, _, share, ranks = product_ref.shape
    return jnp.concatenate([product_ref[:, c].reshape(count * share, ranks) for c in range(2)], 1)


def product_blocks(product):
    chips, cores, share, ranks = product.shape
    return pl.BlockSpec((WIDTH // share, cores, share, ranks), lambda j: (j, 0, 0, 0))


def momentum_update(buffer, left, product):
    rows, columns = buffer.shape

    def kernel(buffer_ref, left_ref, product_ref, out, high, low):
        @pl.when(pl.program_id(0) == 0)
        def _():
            high[...], low[...] = split_two(left_ref[...])

        step = product3((high[...], low[...]), split_two(columns_first(product_ref)), NT)
        out[...] = buffer_ref[...] - decay_keep * step

    half = pltpu.VMEM((rows, R), jnp.bfloat16)
    return call(
        kernel,
        columns // WIDTH,
        (buffer, left, product),
        [wide(rows), whole(rows, R), product_blocks(product)],
        jax.ShapeDtypeStruct((rows, columns), F32),
        wide(rows),
        (half, half),
        name="momentum_update",
    )


def weights_update(weights, ortho, inverse, product, sums, start, share):
    rows, columns = weights.shape
    height = rows + share

    def kernel(start_ref, weights_ref, ortho_ref, inverse_ref, product_ref, sums_ref, out, own, high, low):
        @pl.when(pl.program_id(0) == 0)
        def _():
            scale = jnp.sqrt(jnp.sum(sums_ref[...], axis=0) / N + eps_norm)
            at = pl.multiple_of(start_ref[0], share)
            lanes = lax.broadcasted_iota(jnp.int32, (share, R), 1)
            mine = lanes == at + lax.broadcasted_iota(jnp.int32, (share, R), 0)
            picked = jnp.sum(jnp.where(mine, jnp.broadcast_to(scale, (share, R)), 0.0), axis=1, keepdims=True)
            left = product3(split_two(ortho_ref[...] / scale), split_two(inverse_ref[...]), NN)
            stack = jnp.concatenate([left, inverse_ref[pl.ds(at, share), :] / picked], 0)
            high[...], low[...] = split_two(stack)

        both = product3((high[...], low[...]), split_two(columns_first(product_ref)), NT)
        out[...] = weights_ref[...] - step_size * both[:rows]
        own[...] = both[rows:]

    half = pltpu.VMEM((height, R), jnp.bfloat16)
    return call(
        kernel,
        columns // WIDTH,
        (start, weights, ortho, inverse, product, sums),
        [
            pl.BlockSpec(memory_space=pltpu.SMEM),
            wide(rows),
            whole(rows, R),
            whole(R, R),
            product_blocks(product),
            whole(*sums.shape),
        ],
        (jax.ShapeDtypeStruct((rows, columns), F32), jax.ShapeDtypeStruct((share, columns), F32)),
        (wide(rows), wide(share)),
        (half, half),
        name="weights_update",
    )


SIZES = {"z": Z, "core": 2, "x": 4, "y": 4}


def shift(values, axis, by):
    size = SIZES[axis]
    return lax.ppermute(values, axis, [(i, (i + by) % size) for i in range(size)])


def spread(values, axes, count):
    whole = jnp.broadcast_to(values[None], (count,) + values.shape)
    return lax.all_to_all(whole, axes, 0, 0, tiled=True)


def gather_z(own):
    half = own.shape[0] // 2
    below1, above1 = shift(own, "z", 1), shift(own, "z", -1)
    below2, above2 = shift(own, "z", 2), shift(own, "z", -2)
    below3, above3 = shift(below2, "z", 1), shift(above2, "z", -1)
    across = (shift(below2[:half], "z", 2), shift(above2[half:], "z", -2))
    return [own, above1, above2, above3, across, below3, below2, below1]


def dot(first, second, dims, precision):
    return lax.dot_general(
        first, second, ((dims[0], dims[1]), ((), ())), precision=precision, preferred_element_type=F32
    )


def local(weights, momentum, gradient, right_factor):
    core = lax.axis_index("core")
    plane = lax.axis_index("x") * 4 + lax.axis_index("y")
    z = lax.axis_index("z")
    share = right_factor.shape[0]

    buffer = momentum + gradient.astype(F32)
    right = gather_z(right_factor)
    beside = shift(buffer, "core", 1)
    chip = jnp.where(
        core == 0, jnp.concatenate([buffer, beside], 0), jnp.concatenate([beside, buffer], 0)
    )

    blocks = [*right[:4], *right[4], *right[5:]]
    part = left_product(blocks, chip)
    rows = part.shape[1]
    pieces = lax.all_to_all(part.reshape(XY, -1, rows), ("x", "y"), 0, 0, tiled=True)
    left = spread(jnp.sum(pieces, 0), ("x", "y"), XY).reshape(Z, share, rows)
    own = lax.dynamic_slice_in_dim(jnp.concatenate([left, left], 0), (Z - z) % Z, Z, 0)

    product = right_product(own.reshape(Z * share, rows), chip)
    product = lax.psum_scatter(product, "z", scatter_dimension=0, tiled=True)

    other = shift(own, "core", 1)
    by_core = [jnp.where(core == 0, own, other), jnp.where(core == 0, other, own)]
    left_all = jnp.stack(by_core, 1).reshape(R, rows)
    height = R // (2 * XY)
    mine = lax.dynamic_slice_in_dim(left_all, (core * XY + plane) * height, height, 0)
    gram = jnp.sum(spread(dot(mine, left_all, ((1,), (1,)), HIGHEST), "z", Z), 0)
    gram = spread(gram, ("x", "y"), XY).reshape(R // 2, R)
    gram_other = shift(gram, "core", 1)
    gram = jnp.where(
        core == 0, jnp.concatenate([gram, gram_other], 0), jnp.concatenate([gram_other, gram], 0)
    )
    product = after(product, gram)
    inverse = inverse_factor(gram, product)

    beside = shift(product, "core", 1)
    sums = column_squares(inverse, product, beside, jnp.full((1,), core, jnp.int32))
    sums = lax.all_to_all(sums, "z", 0, 0, tiled=True)
    product = lax.all_gather(product, ("z", "core"), axis=0, tiled=True)
    product = product.reshape(Z, 2, -1, product.shape[1])

    height = rows // 2
    left_own = jnp.concatenate(by_core, 0).reshape(R, rows)
    left_own = jnp.where(core == 0, left_own[:, :height], left_own[:, height:])
    ortho = dot(left_own, inverse, ((0,), (1,)), HIGHEST)
    sums = lax.all_to_all(total_after(sums, product), ("x", "y"), 0, 0, tiled=True)
    new_momentum = momentum_update(buffer, dot(ortho, inverse, NN, HIGHEST), product)
    start = jnp.full((1,), (2 * z + core) * share, jnp.int32)
    new_weights, new_right = weights_update(weights, ortho, inverse, product, sums, start, share)
    return (new_weights, new_momentum, new_right)


def solution(mesh):
    fine = Mesh(mesh.devices.reshape(Z, 2, 4, 4), ("z", "core", "x", "y"))
    spec = P(("z", "core"), ("x", "y"))
    return jax.shard_map(
        local, mesh=fine, in_specs=(spec, spec, spec, spec), out_specs=(spec, spec, spec), check_vma=False
    )
```

```python
import jax
import jax.numpy as jnp
from jax import lax
from jax.experimental import pallas as pl
from jax.experimental.pallas import tpu as pltpu
from jax.sharding import Mesh, PartitionSpec as P

N = 28672
R = 512
Z = 8
XY = 16
TILE = 128

decay_keep = 0.05
step_size = 0.5
eps_norm = 1e-06

LIMIT = 52 * 2**20
F32 = jnp.float32
HIGHEST = lax.Precision.HIGHEST


def split_three(values):
    high = values.astype(jnp.bfloat16).astype(F32)
    rest = values - high
    middle = rest.astype(jnp.bfloat16).astype(F32)
    low = (rest - middle).astype(jnp.bfloat16).astype(F32)
    return high, middle, low


def invert_factor_8(entries):
    size = len(entries)
    left = [row[:] for row in entries]
    inverse = [[None] * size for _ in range(size)]
    for j in range(size):
        root = lax.rsqrt(left[j][j])
        square = root * root
        for i in range(j + 1, size):
            share = left[i][j] * square
            for k in range(j + 1, i + 1):
                left[i][k] = left[i][k] - share * left[k][j]
        column = [None] * size
        for i in range(j + 1, size):
            column[i] = left[i][j] * root
        for c in range(j):
            inverse[j][c] = inverse[j][c] * root
        inverse[j][j] = root
        for i in range(j + 1, size):
            for c in range(j + 1):
                term = column[i] * inverse[j][c]
                inverse[i][c] = -term if inverse[i][c] is None else inverse[i][c] - term
    return inverse


def invert_factor_tile(state, result):
    sublane = lax.broadcasted_iota(jnp.int32, (8, TILE), 0)
    lane = lax.broadcasted_iota(jnp.int32, (8, TILE), 1)
    rows = state[0:8, :]
    for step in range(TILE // 8):
        at = 8 * step
        lanes = [jnp.broadcast_to(rows[:, at + j : at + j + 1], (8, TILE)) for j in range(8)]
        entries = [
            [jnp.broadcast_to(lanes[j][i : i + 1, :], (8, TILE)) for j in range(i + 1)] for i in range(8)
        ]
        inverse = invert_factor_8(entries)
        first, second = None, None
        for j in range(8):
            column = jnp.zeros((8, TILE), F32)
            for i in range(j, 8):
                column = jnp.where(sublane == i, inverse[i][j], column)
            one = column * jnp.broadcast_to(rows[j : j + 1, :TILE], (8, TILE))
            two = column * jnp.broadcast_to(rows[j : j + 1, TILE:], (8, TILE))
            first = one if first is None else first + one
            second = two if second is None else second + two
        result[at : at + 8, :] = second
        after = at + 8
        if after == TILE:
            break
        next_first, next_second = state[after : after + 8, :TILE], state[after : after + 8, TILE:]
        for k in range(8):
            one = jnp.broadcast_to(first[k : k + 1, :], (8, TILE))
            two = jnp.broadcast_to(second[k : k + 1, :], (8, TILE))
            factor = jnp.sum(jnp.where(lane == after + sublane, one, 0.0), axis=1, keepdims=True)
            next_first, next_second = next_first - factor * one, next_second - factor * two
        rows = jnp.concatenate([next_first, next_second], 1)
        if after + 8 < TILE:
            high, middle, low = split_three(jnp.concatenate([first, second], 1))
            right = jnp.concatenate([high, middle, high, low, high, middle], 0).astype(jnp.bfloat16)
            high, middle, low = high[:, :TILE], middle[:, :TILE], low[:, :TILE]
            left = jnp.concatenate([high, high, middle, high, low, middle], 0).astype(jnp.bfloat16)
            update = lax.dot_general(left, right, (((0,), (0,)), ((), ())), preferred_element_type=F32)
            state[after + 8 :, :] = state[after + 8 :, :] - update[after + 8 :, :]


def inverse_factor_kernel(gram, earlier, result, inverse, rest, state, tile):
    rows = lax.broadcasted_iota(jnp.int32, (R, R), 0)
    columns = lax.broadcasted_iota(jnp.int32, (R, R), 1)
    rest[...] = gram[...]
    inverse[...] = jnp.where(rows == columns, 1.0, 0.0)
    identity = jnp.where(
        lax.broadcasted_iota(jnp.int32, (TILE, TILE), 0) == lax.broadcasted_iota(jnp.int32, (TILE, TILE), 1), 1.0, 0.0
    )

    def eliminate(k):
        here, left, right = slice(k * TILE, (k + 1) * TILE), slice(0, (k + 1) * TILE), slice((k + 1) * TILE, R)
        lower = jnp.dot(tile[...], inverse[here, left], precision=HIGHEST, preferred_element_type=F32)
        inverse[here, left] = lower
        if k == R // TILE - 1:
            return
        upper = jnp.dot(tile[...], rest[here, right], precision=HIGHEST, preferred_element_type=F32)
        dims = (((0,), (0,)), ((), ()))
        for i in range(k + 1, R // TILE):
            below = slice(i * TILE, (i + 1) * TILE)
            skip = (i - k - 1) * TILE
            factor = upper[:, skip : skip + TILE]
            rest[below, below.start :] -= lax.dot_general(
                factor, upper[:, skip:], dims, precision=HIGHEST, preferred_element_type=F32
            )
            inverse[below, left] -= lax.dot_general(factor, lower, dims, precision=HIGHEST, preferred_element_type=F32)

    @pl.loop(0, R // TILE)
    def _(k):
        at = pl.multiple_of(k * TILE, TILE)
        state[:, :TILE] = rest[pl.ds(at, TILE), pl.ds(at, TILE)]
        state[:, TILE:] = identity
        invert_factor_tile(state, tile)
        for done in range(R // TILE):

            @pl.when(k == done)
            def _():
                eliminate(done)

    share = R // (2 * Z)
    core, chip, place = columns // (R // 2), columns // share % Z, columns % share
    chosen = jnp.where(rows == (2 * chip + core) * share + place, 1.0, 0.0).astype(jnp.bfloat16)
    parts = [part.astype(jnp.bfloat16) for part in split_three(inverse[...])]
    high, middle, low = (jnp.dot(part, chosen, preferred_element_type=F32) for part in parts)
    result[...] = high + (middle + low)


def inverse_factor(gram, earlier):
    whole = pl.BlockSpec(memory_space=pltpu.VMEM)
    return pl.pallas_call(
        inverse_factor_kernel,
        out_shape=jax.ShapeDtypeStruct((R, R), F32),
        in_specs=[whole, pl.BlockSpec(memory_space=pl.ANY)],
        out_specs=whole,
        scratch_shapes=[
            pltpu.VMEM((R, R), F32),
            pltpu.VMEM((R, R), F32),
            pltpu.VMEM((TILE, 2 * TILE), F32),
            pltpu.VMEM((TILE, TILE), F32),
        ],
        compiler_params=pltpu.CompilerParams(vmem_limit_bytes=12 * 2**20),
        cost_estimate=pl.CostEstimate(flops=3 * 10**10, bytes_accessed=2 * 4 * R * R, transcendentals=R),
        name="inverse_factor",
    )(gram, earlier)


def after(values, earlier):
    tile = (slice(0, 8), slice(0, 128))
    first = jnp.where(earlier[tile] == earlier[tile], values[tile], earlier[tile])
    return lax.dynamic_update_slice(values, first, (0, 0))


def split_two(values):
    high = values.astype(jnp.bfloat16)
    return high, (values - high.astype(F32)).astype(jnp.bfloat16)


def product3(first, second, dims):
    def one(a, b):
        return lax.dot_general(a, b, (dims, ((), ())), preferred_element_type=F32)

    return one(first[0], second[0]) + (one(first[0], second[1]) + one(first[1], second[0]))


WIDTH = 896
NN = ((1,), (0,))
NT = ((1,), (1,))


def call(kernel, steps, operands, specs, outs, out_specs, scratch=(), name=None, flops=3 * 10**9, limit=LIMIT):
    return pl.pallas_call(
        kernel,
        grid=(steps,),
        out_shape=outs,
        in_specs=specs,
        out_specs=out_specs,
        scratch_shapes=list(scratch),
        compiler_params=pltpu.CompilerParams(vmem_limit_bytes=limit, dimension_semantics=("arbitrary",)),
        cost_estimate=pl.CostEstimate(flops=flops, bytes_accessed=4 * 2**20, transcendentals=0),
        name=name,
    )(*operands)


def wide(rows):
    return pl.BlockSpec((rows, WIDTH), lambda j: (0, j))


def whole(*shape):
    return pl.BlockSpec(shape, lambda j: (0,) * len(shape))


def left_product(blocks, chip):
    rows, columns = chip.shape
    ranks = sum(b.shape[0] for b in blocks)

    def kernel(*refs):
        parts, chip_ref, out = refs[:-2], refs[-2], refs[-1]
        right = jnp.concatenate([p[...] for p in parts], 0)
        term = product3(split_two(right), split_two(chip_ref[...]), NT)

        @pl.when(pl.program_id(0) == 0)
        def _():
            out[...] = term

        @pl.when(pl.program_id(0) > 0)
        def _():
            out[...] += term

    return call(
        kernel,
        columns // WIDTH,
        (*blocks, chip),
        [wide(b.shape[0]) for b in blocks] + [wide(rows)],
        jax.ShapeDtypeStruct((ranks, rows), F32),
        whole(ranks, rows),
        name="left_product",
        limit=16 * 2**20,
    )


def right_product(left, chip):
    ranks, rows = left.shape
    columns = chip.shape[1]

    def kernel(left_ref, chip_ref, out, high, low):
        @pl.when(pl.program_id(0) == 0)
        def _():
            high[...], low[...] = split_two(left_ref[...])

        out[...] = product3((high[...], low[...]), split_two(chip_ref[...]), NN).T

    half = pltpu.VMEM((ranks, rows), jnp.bfloat16)
    return call(
        kernel,
        columns // WIDTH,
        (left, chip),
        [whole(ranks, rows), wide(rows)],
        jax.ShapeDtypeStruct((columns, ranks), F32),
        pl.BlockSpec((WIDTH, ranks), lambda j: (j, 0)),
        (half, half),
        name="right_product",
    )


def column_squares(inverse, own, other, core):
    def kernel(core_ref, inverse_ref, own_ref, other_ref, sums):
        mine = core_ref[0] == 0
        first = jnp.where(mine, own_ref[...], other_ref[...])
        second = jnp.where(mine, other_ref[...], own_ref[...])
        product = jnp.concatenate([first, second], 1)
        right = product3(split_two(product), split_two(inverse_ref[...]), NT)
        sums[...] = jnp.broadcast_to(jnp.sum(right * right, axis=0, keepdims=True), sums.shape)

    vmem = pl.BlockSpec(memory_space=pltpu.VMEM)
    return pl.pallas_call(
        kernel,
        out_shape=jax.ShapeDtypeStruct((Z, 1, R), F32),
        in_specs=[pl.BlockSpec(memory_space=pltpu.SMEM), vmem, vmem, vmem],
        out_specs=vmem,
        compiler_params=pltpu.CompilerParams(vmem_limit_bytes=16 * 2**20),
        cost_estimate=pl.CostEstimate(flops=10**9, bytes_accessed=2**20, transcendentals=0),
        name="column_squares",
    )(core, inverse, own, other)


def columns_first(product_ref):
    count, _, share, ranks = product_ref.shape
    return jnp.concatenate([product_ref[:, c].reshape(count * share, ranks) for c in range(2)], 1)


def product_blocks(product):
    chips, cores, share, ranks = product.shape
    return pl.BlockSpec((WIDTH // share, cores, share, ranks), lambda j: (j, 0, 0, 0))


def update(weights, buffer, ortho, inverse, product, sums, start, share):
    rows, columns = weights.shape
    height = 2 * rows + share

    def kernel(
        start_ref, weights_ref, buffer_ref, ortho_ref, inverse_ref, product_ref, sums_ref,
        new_weights, new_momentum, own, high, low,
    ):
        @pl.when(pl.program_id(0) == 0)
        def _():
            scale = jnp.sqrt(jnp.sum(sums_ref[...], axis=0) / N + eps_norm)
            at = pl.multiple_of(start_ref[0], share)
            lanes = lax.broadcasted_iota(jnp.int32, (share, R), 1)
            mine = lanes == at + lax.broadcasted_iota(jnp.int32, (share, R), 0)
            picked = jnp.sum(jnp.where(mine, jnp.broadcast_to(scale, (share, R)), 0.0), axis=1, keepdims=True)
            both = jnp.concatenate([ortho_ref[...], ortho_ref[...] / scale], 0)
            left = product3(split_two(both), split_two(inverse_ref[...]), NN)
            stack = jnp.concatenate([left, inverse_ref[pl.ds(at, share), :] / picked], 0)
            high[...], low[...] = split_two(stack)

        steps = product3((high[...], low[...]), split_two(columns_first(product_ref)), NT)
        new_momentum[...] = buffer_ref[...] - decay_keep * steps[:rows]
        new_weights[...] = weights_ref[...] - step_size * steps[rows : 2 * rows]
        own[...] = steps[2 * rows :]

    full = jax.ShapeDtypeStruct((rows, columns), F32)
    stacked = pltpu.VMEM((height, R), jnp.bfloat16)
    return call(
        kernel,
        columns // WIDTH,
        (start, weights, buffer, ortho, inverse, product, sums),
        [
            pl.BlockSpec(memory_space=pltpu.SMEM),
            wide(rows),
            wide(rows),
            whole(rows, R),
            whole(R, R),
            product_blocks(product),
            whole(*sums.shape),
        ],
        (full, full, jax.ShapeDtypeStruct((share, columns), F32)),
        (wide(rows), wide(rows), wide(share)),
        (stacked, stacked),
        name="update",
    )


SIZES = {"z": Z, "core": 2, "x": 4, "y": 4}


def shift(values, axis, by):
    size = SIZES[axis]
    return lax.ppermute(values, axis, [(i, (i + by) % size) for i in range(size)])


def spread(values, axes, count):
    whole = jnp.broadcast_to(values[None], (count,) + values.shape)
    return lax.all_to_all(whole, axes, 0, 0, tiled=True)


def gather_z(own):
    half = own.shape[0] // 2
    below1, above1 = shift(own, "z", 1), shift(own, "z", -1)
    below2, above2 = shift(own, "z", 2), shift(own, "z", -2)
    below3, above3 = shift(below2, "z", 1), shift(above2, "z", -1)
    across = (shift(below2[:half], "z", 2), shift(above2[half:], "z", -2))
    return [own, above1, above2, above3, across, below3, below2, below1]


def dot(first, second, dims, precision):
    return lax.dot_general(
        first, second, ((dims[0], dims[1]), ((), ())), precision=precision, preferred_element_type=F32
    )


def local(weights, momentum, gradient, right_factor):
    core = lax.axis_index("core")
    plane = lax.axis_index("x") * 4 + lax.axis_index("y")
    z = lax.axis_index("z")
    share = right_factor.shape[0]

    buffer = momentum + gradient.astype(F32)
    right = gather_z(right_factor)
    beside = shift(buffer, "core", 1)
    chip = jnp.where(
        core == 0, jnp.concatenate([buffer, beside], 0), jnp.concatenate([beside, buffer], 0)
    )

    blocks = [*right[:4], *right[4], *right[5:]]
    part = left_product(blocks, chip)
    rows = part.shape[1]
    pieces = lax.all_to_all(part.reshape(XY, -1, rows), ("x", "y"), 0, 0, tiled=True)
    left = spread(jnp.sum(pieces, 0), ("x", "y"), XY).reshape(Z, share, rows)
    own = lax.dynamic_slice_in_dim(jnp.concatenate([left, left], 0), (Z - z) % Z, Z, 0)

    product = right_product(own.reshape(Z * share, rows), chip)
    product = lax.psum_scatter(product, "z", scatter_dimension=0, tiled=True)

    other = shift(own, "core", 1)
    by_core = [jnp.where(core == 0, own, other), jnp.where(core == 0, other, own)]
    left_all = jnp.stack(by_core, 1).reshape(R, rows)
    height = R // (2 * XY)
    mine = lax.dynamic_slice_in_dim(left_all, (core * XY + plane) * height, height, 0)
    gram = jnp.sum(spread(dot(mine, left_all, ((1,), (1,)), HIGHEST), "z", Z), 0)
    gram = spread(gram, ("x", "y"), XY).reshape(R // 2, R)
    gram_other = shift(gram, "core", 1)
    gram = jnp.where(
        core == 0, jnp.concatenate([gram, gram_other], 0), jnp.concatenate([gram_other, gram], 0)
    )
    product = after(product, gram)
    inverse = inverse_factor(gram, product)

    beside = shift(product, "core", 1)
    sums = column_squares(inverse, product, beside, jnp.full((1,), core, jnp.int32))
    sums = lax.all_to_all(sums, "z", 0, 0, tiled=True)
    product = lax.all_gather(product, ("z", "core"), axis=0, tiled=True)
    product = product.reshape(Z, 2, -1, product.shape[1])

    height = rows // 2
    left_own = jnp.concatenate(by_core, 0).reshape(R, rows)
    left_own = jnp.where(core == 0, left_own[:, :height], left_own[:, height:])
    ortho = dot(left_own, inverse, ((0,), (1,)), HIGHEST)
    sums = spread(jnp.sum(sums, 0), ("x", "y"), XY)
    start = jnp.full((1,), (2 * z + core) * share, jnp.int32)
    new_weights, new_momentum, new_right = update(weights, buffer, ortho, inverse, product, sums, start, share)
    return (new_weights, new_momentum, new_right)


def solution(mesh):
    fine = Mesh(mesh.devices.reshape(Z, 2, 4, 4), ("z", "core", "x", "y"))
    spec = P(("z", "core"), ("x", "y"))
    return jax.shard_map(
        local, mesh=fine, in_specs=(spec, spec, spec, spec), out_specs=(spec, spec, spec), check_vma=False
    )
```

```python
import jax
import jax.numpy as jnp
from jax import lax
from jax.experimental import pallas as pl
from jax.experimental.pallas import tpu as pltpu
from jax.sharding import Mesh, PartitionSpec as P

N = 28672
R = 512
Z = 8
XY = 16
TILE = 128

decay_keep = 0.05
step_size = 0.5
eps_norm = 1e-06

LIMIT = 52 * 2**20
F32 = jnp.float32
HIGHEST = lax.Precision.HIGHEST


def split_three(values):
    high = values.astype(jnp.bfloat16).astype(F32)
    rest = values - high
    middle = rest.astype(jnp.bfloat16).astype(F32)
    low = (rest - middle).astype(jnp.bfloat16).astype(F32)
    return high, middle, low


def invert_factor_8(entries):
    size = len(entries)
    left = [row[:] for row in entries]
    inverse = [[None] * size for _ in range(size)]
    for j in range(size):
        root = lax.rsqrt(left[j][j])
        square = root * root
        for i in range(j + 1, size):
            share = left[i][j] * square
            for k in range(j + 1, i + 1):
                left[i][k] = left[i][k] - share * left[k][j]
        column = [None] * size
        for i in range(j + 1, size):
            column[i] = left[i][j] * root
        for c in range(j):
            inverse[j][c] = inverse[j][c] * root
        inverse[j][j] = root
        for i in range(j + 1, size):
            for c in range(j + 1):
                term = column[i] * inverse[j][c]
                inverse[i][c] = -term if inverse[i][c] is None else inverse[i][c] - term
    return inverse


def invert_factor_tile(state, result):
    sublane = lax.broadcasted_iota(jnp.int32, (8, TILE), 0)
    lane = lax.broadcasted_iota(jnp.int32, (8, TILE), 1)
    rows = state[0:8, :]
    for step in range(TILE // 8):
        at = 8 * step
        lanes = [jnp.broadcast_to(rows[:, at + j : at + j + 1], (8, TILE)) for j in range(8)]
        entries = [
            [jnp.broadcast_to(lanes[j][i : i + 1, :], (8, TILE)) for j in range(i + 1)] for i in range(8)
        ]
        inverse = invert_factor_8(entries)
        first, second = None, None
        for j in range(8):
            column = jnp.zeros((8, TILE), F32)
            for i in range(j, 8):
                column = jnp.where(sublane == i, inverse[i][j], column)
            one = column * jnp.broadcast_to(rows[j : j + 1, :TILE], (8, TILE))
            two = column * jnp.broadcast_to(rows[j : j + 1, TILE:], (8, TILE))
            first = one if first is None else first + one
            second = two if second is None else second + two
        result[at : at + 8, :] = second
        after = at + 8
        if after == TILE:
            break
        next_first, next_second = state[after : after + 8, :TILE], state[after : after + 8, TILE:]
        for k in range(8):
            one = jnp.broadcast_to(first[k : k + 1, :], (8, TILE))
            two = jnp.broadcast_to(second[k : k + 1, :], (8, TILE))
            factor = jnp.sum(jnp.where(lane == after + sublane, one, 0.0), axis=1, keepdims=True)
            next_first, next_second = next_first - factor * one, next_second - factor * two
        rows = jnp.concatenate([next_first, next_second], 1)
        if after + 8 < TILE:
            high, middle, low = split_three(jnp.concatenate([first, second], 1))
            right = jnp.concatenate([high, middle, high, low, high, middle], 0).astype(jnp.bfloat16)
            high, middle, low = high[:, :TILE], middle[:, :TILE], low[:, :TILE]
            left = jnp.concatenate([high, high, middle, high, low, middle], 0).astype(jnp.bfloat16)
            update = lax.dot_general(left, right, (((0,), (0,)), ((), ())), preferred_element_type=F32)
            state[after + 8 :, :] = state[after + 8 :, :] - update[after + 8 :, :]


def inverse_factor_kernel(gram, earlier, result, inverse, rest, state, tile):
    rows = lax.broadcasted_iota(jnp.int32, (R, R), 0)
    columns = lax.broadcasted_iota(jnp.int32, (R, R), 1)
    rest[...] = gram[...]
    inverse[...] = jnp.where(rows == columns, 1.0, 0.0)
    identity = jnp.where(
        lax.broadcasted_iota(jnp.int32, (TILE, TILE), 0) == lax.broadcasted_iota(jnp.int32, (TILE, TILE), 1), 1.0, 0.0
    )

    def eliminate(k):
        here, left, right = slice(k * TILE, (k + 1) * TILE), slice(0, (k + 1) * TILE), slice((k + 1) * TILE, R)
        lower = jnp.dot(tile[...], inverse[here, left], precision=HIGHEST, preferred_element_type=F32)
        inverse[here, left] = lower
        if k == R // TILE - 1:
            return
        upper = jnp.dot(tile[...], rest[here, right], precision=HIGHEST, preferred_element_type=F32)
        dims = (((0,), (0,)), ((), ()))
        for i in range(k + 1, R // TILE):
            below = slice(i * TILE, (i + 1) * TILE)
            skip = (i - k - 1) * TILE
            factor = upper[:, skip : skip + TILE]
            rest[below, below.start :] -= lax.dot_general(
                factor, upper[:, skip:], dims, precision=HIGHEST, preferred_element_type=F32
            )
            inverse[below, left] -= lax.dot_general(factor, lower, dims, precision=HIGHEST, preferred_element_type=F32)

    @pl.loop(0, R // TILE)
    def _(k):
        at = pl.multiple_of(k * TILE, TILE)
        state[:, :TILE] = rest[pl.ds(at, TILE), pl.ds(at, TILE)]
        state[:, TILE:] = identity
        invert_factor_tile(state, tile)
        for done in range(R // TILE):

            @pl.when(k == done)
            def _():
                eliminate(done)

    share = R // (2 * Z)
    core, chip, place = columns // (R // 2), columns // share % Z, columns % share
    chosen = jnp.where(rows == (2 * chip + core) * share + place, 1.0, 0.0).astype(jnp.bfloat16)
    parts = [part.astype(jnp.bfloat16) for part in split_three(inverse[...])]
    high, middle, low = (jnp.dot(part, chosen, preferred_element_type=F32) for part in parts)
    result[...] = high + (middle + low)


def inverse_factor(gram, earlier):
    whole = pl.BlockSpec(memory_space=pltpu.VMEM)
    return pl.pallas_call(
        inverse_factor_kernel,
        out_shape=jax.ShapeDtypeStruct((R, R), F32),
        in_specs=[whole, pl.BlockSpec(memory_space=pl.ANY)],
        out_specs=whole,
        scratch_shapes=[
            pltpu.VMEM((R, R), F32),
            pltpu.VMEM((R, R), F32),
            pltpu.VMEM((TILE, 2 * TILE), F32),
            pltpu.VMEM((TILE, TILE), F32),
        ],
        compiler_params=pltpu.CompilerParams(vmem_limit_bytes=12 * 2**20),
        cost_estimate=pl.CostEstimate(flops=3 * 10**10, bytes_accessed=2 * 4 * R * R, transcendentals=R),
        name="inverse_factor",
    )(gram, earlier)


def after(values, earlier):
    tile = (slice(0, 8), slice(0, 128))
    first = jnp.where(earlier[tile] == earlier[tile], values[tile], earlier[tile])
    return lax.dynamic_update_slice(values, first, (0, 0))


def split_two(values):
    high = values.astype(jnp.bfloat16)
    return high, (values - high.astype(F32)).astype(jnp.bfloat16)


def product3(first, second, dims):
    def one(a, b):
        return lax.dot_general(a, b, (dims, ((), ())), preferred_element_type=F32)

    return one(first[0], second[0]) + (one(first[0], second[1]) + one(first[1], second[0]))


WIDTH = 896
NN = ((1,), (0,))
NT = ((1,), (1,))


def call(kernel, steps, operands, specs, outs, out_specs, scratch=(), name=None, flops=3 * 10**9, limit=LIMIT):
    return pl.pallas_call(
        kernel,
        grid=(steps,),
        out_shape=outs,
        in_specs=specs,
        out_specs=out_specs,
        scratch_shapes=list(scratch),
        compiler_params=pltpu.CompilerParams(vmem_limit_bytes=limit, dimension_semantics=("arbitrary",)),
        cost_estimate=pl.CostEstimate(flops=flops, bytes_accessed=4 * 2**20, transcendentals=0),
        name=name,
    )(*operands)


def wide(rows):
    return pl.BlockSpec((rows, WIDTH), lambda j: (0, j))


def whole(*shape):
    return pl.BlockSpec(shape, lambda j: (0,) * len(shape))


def left_product(blocks, chip):
    rows, columns = chip.shape
    ranks = sum(b.shape[0] for b in blocks)

    def kernel(*refs):
        parts, chip_ref, out = refs[:-2], refs[-2], refs[-1]
        right = jnp.concatenate([p[...] for p in parts], 0)
        term = product3(split_two(right), split_two(chip_ref[...]), NT)

        @pl.when(pl.program_id(0) == 0)
        def _():
            out[...] = term

        @pl.when(pl.program_id(0) > 0)
        def _():
            out[...] += term

    return call(
        kernel,
        columns // WIDTH,
        (*blocks, chip),
        [wide(b.shape[0]) for b in blocks] + [wide(rows)],
        jax.ShapeDtypeStruct((ranks, rows), F32),
        whole(ranks, rows),
        name="left_product",
        limit=16 * 2**20,
    )


def right_product(left, chip):
    ranks, rows = left.shape
    columns = chip.shape[1]

    def kernel(left_ref, chip_ref, out, high, low):
        @pl.when(pl.program_id(0) == 0)
        def _():
            high[...], low[...] = split_two(left_ref[...])

        out[...] = product3((high[...], low[...]), split_two(chip_ref[...]), NN).T

    half = pltpu.VMEM((ranks, rows), jnp.bfloat16)
    return call(
        kernel,
        columns // WIDTH,
        (left, chip),
        [whole(ranks, rows), wide(rows)],
        jax.ShapeDtypeStruct((columns, ranks), F32),
        pl.BlockSpec((WIDTH, ranks), lambda j: (j, 0)),
        (half, half),
        name="right_product",
    )


def column_squares(inverse, own, other, core):
    def kernel(core_ref, inverse_ref, own_ref, other_ref, sums):
        mine = core_ref[0] == 0
        first = jnp.where(mine, own_ref[...], other_ref[...])
        second = jnp.where(mine, other_ref[...], own_ref[...])
        product = jnp.concatenate([first, second], 1)
        right = product3(split_two(product), split_two(inverse_ref[...]), NT)
        sums[...] = jnp.broadcast_to(jnp.sum(right * right, axis=0, keepdims=True), sums.shape)

    vmem = pl.BlockSpec(memory_space=pltpu.VMEM)
    return pl.pallas_call(
        kernel,
        out_shape=jax.ShapeDtypeStruct((Z, 1, R), F32),
        in_specs=[pl.BlockSpec(memory_space=pltpu.SMEM), vmem, vmem, vmem],
        out_specs=vmem,
        compiler_params=pltpu.CompilerParams(vmem_limit_bytes=16 * 2**20),
        cost_estimate=pl.CostEstimate(flops=10**9, bytes_accessed=2**20, transcendentals=0),
        name="column_squares",
    )(core, inverse, own, other)


def columns_first(product_ref):
    count, _, share, ranks = product_ref.shape
    return jnp.concatenate([product_ref[:, c].reshape(count * share, ranks) for c in range(2)], 1)


def product_blocks(product):
    chips, cores, share, ranks = product.shape
    return pl.BlockSpec((WIDTH // share, cores, share, ranks), lambda j: (j, 0, 0, 0))


def update(weights, buffer, ortho, inverse, product, sums, start, share):
    rows, columns = weights.shape
    height = 2 * rows + share

    def kernel(
        start_ref, weights_ref, buffer_ref, ortho_ref, inverse_ref, product_ref, sums_ref,
        new_weights, new_momentum, own, high, low,
    ):
        @pl.when(pl.program_id(0) == 0)
        def _():
            scale = jnp.sqrt(jnp.sum(sums_ref[...], axis=0) / N + eps_norm)
            at = pl.multiple_of(start_ref[0], share)
            lanes = lax.broadcasted_iota(jnp.int32, (share, R), 1)
            mine = lanes == at + lax.broadcasted_iota(jnp.int32, (share, R), 0)
            picked = jnp.sum(jnp.where(mine, jnp.broadcast_to(scale, (share, R)), 0.0), axis=1, keepdims=True)
            both = jnp.concatenate([ortho_ref[...], ortho_ref[...] / scale], 0)
            left = product3(split_two(both), split_two(inverse_ref[...]), NN)
            stack = jnp.concatenate([left, inverse_ref[pl.ds(at, share), :] / picked], 0)
            high[...], low[...] = split_two(stack)

        steps = product3((high[...], low[...]), split_two(columns_first(product_ref)), NT)
        new_momentum[...] = buffer_ref[...] - decay_keep * steps[:rows]
        new_weights[...] = weights_ref[...] - step_size * steps[rows : 2 * rows]
        own[...] = steps[2 * rows :]

    full = jax.ShapeDtypeStruct((rows, columns), F32)
    stacked = pltpu.VMEM((height, R), jnp.bfloat16)
    return call(
        kernel,
        columns // WIDTH,
        (start, weights, buffer, ortho, inverse, product, sums),
        [
            pl.BlockSpec(memory_space=pltpu.SMEM),
            wide(rows),
            wide(rows),
            whole(rows, R),
            whole(R, R),
            product_blocks(product),
            whole(*sums.shape),
        ],
        (full, full, jax.ShapeDtypeStruct((share, columns), F32)),
        (wide(rows), wide(rows), wide(share)),
        (stacked, stacked),
        name="update",
    )


SIZES = {"z": Z, "core": 2, "x": 4, "y": 4}


def shift(values, axis, by):
    size = SIZES[axis]
    return lax.ppermute(values, axis, [(i, (i + by) % size) for i in range(size)])


def spread(values, axes, count):
    whole = jnp.broadcast_to(values[None], (count,) + values.shape)
    return lax.all_to_all(whole, axes, 0, 0, tiled=True)


def gather_z(own):
    half = own.shape[0] // 2
    below1, above1 = shift(own, "z", 1), shift(own, "z", -1)
    below2, above2 = shift(own, "z", 2), shift(own, "z", -2)
    below3, above3 = shift(below2, "z", 1), shift(above2, "z", -1)
    across = (shift(below2[:half], "z", 2), shift(above2[half:], "z", -2))
    return [own, above1, above2, above3, across, below3, below2, below1]


def dot(first, second, dims, precision):
    return lax.dot_general(
        first, second, ((dims[0], dims[1]), ((), ())), precision=precision, preferred_element_type=F32
    )


def local(weights, momentum, gradient, right_factor):
    core = lax.axis_index("core")
    plane = lax.axis_index("x") * 4 + lax.axis_index("y")
    z = lax.axis_index("z")
    share = right_factor.shape[0]

    buffer = momentum + gradient.astype(F32)
    right = gather_z(right_factor)
    beside = shift(buffer, "core", 1)
    chip = jnp.where(
        core == 0, jnp.concatenate([buffer, beside], 0), jnp.concatenate([beside, buffer], 0)
    )

    blocks = [*right[:4], *right[4], *right[5:]]
    part = left_product(blocks, chip)
    rows = part.shape[1]
    pieces = lax.all_to_all(part.reshape(XY, -1, rows), ("x", "y"), 0, 0, tiled=True)
    left = spread(jnp.sum(pieces, 0), ("x", "y"), XY).reshape(Z, share, rows)
    own = lax.dynamic_slice_in_dim(jnp.concatenate([left, left], 0), (Z - z) % Z, Z, 0)

    product = right_product(own.reshape(Z * share, rows), chip)
    product = lax.psum_scatter(product, "z", scatter_dimension=0, tiled=True)

    other = shift(own, "core", 1)
    by_core = [jnp.where(core == 0, own, other), jnp.where(core == 0, other, own)]
    left_all = jnp.stack(by_core, 1).reshape(R, rows)
    height = R // (2 * XY)
    mine = lax.dynamic_slice_in_dim(left_all, (core * XY + plane) * height, height, 0)
    gram = jnp.sum(spread(dot(mine, left_all, ((1,), (1,)), HIGHEST), "z", Z), 0)
    gram = spread(gram, ("x", "y"), XY).reshape(R // 2, R)
    gram_other = shift(gram, "core", 1)
    gram = jnp.where(
        core == 0, jnp.concatenate([gram, gram_other], 0), jnp.concatenate([gram_other, gram], 0)
    )
    product = after(product, gram)
    inverse = inverse_factor(gram, product[:8, :128])

    beside = shift(product, "core", 1)
    sums = column_squares(inverse, product, beside, jnp.full((1,), core, jnp.int32))
    sums = lax.all_to_all(sums, "z", 0, 0, tiled=True)
    product = lax.all_gather(product, ("z", "core"), axis=0, tiled=True)
    product = product.reshape(Z, 2, -1, product.shape[1])

    height = rows // 2
    left_own = jnp.concatenate(by_core, 0).reshape(R, rows)
    left_own = jnp.where(core == 0, left_own[:, :height], left_own[:, height:])
    ortho = dot(left_own, inverse, ((0,), (1,)), HIGHEST)
    sums = spread(jnp.sum(sums, 0), ("x", "y"), XY)
    start = jnp.full((1,), (2 * z + core) * share, jnp.int32)
    new_weights, new_momentum, new_right = update(weights, buffer, ortho, inverse, product, sums, start, share)
    return (new_weights, new_momentum, new_right)


def solution(mesh):
    fine = Mesh(mesh.devices.reshape(Z, 2, 4, 4), ("z", "core", "x", "y"))
    spec = P(("z", "core"), ("x", "y"))
    return jax.shard_map(
        local, mesh=fine, in_specs=(spec, spec, spec, spec), out_specs=(spec, spec, spec), check_vma=False
    )
```
